32 devices in a mesh: ctx: 8 (over z, y), head: 4 (over x, core).
Axes of the slice: x: 2, y: 2, z: 4, core: 2. Of those that a mesh axis runs over, the one named last changes fastest.
Arguments:
- queries: bfloat16 [1024, 32, 128], P('ctx', 'head'), may hold values from -70 to 70
- keys: bfloat16 [1024, 32, 128], P('ctx', 'head'), may hold values from -6 to 6
- values: bfloat16 [1024, 32, 128], P('ctx', 'head'), may hold values from -6 to 6
- teacher: bfloat16 [1024, 32, 128], P('ctx', 'head'), may hold values from -18 to 18
- wq: bfloat16 [32, 64, 128], P('head'), may hold values from -0.5 to 0.5
- wk: bfloat16 [32, 64, 128], P('head'), may hold values from -0.5 to 0.5
Outputs:
- student: bfloat16 [1024, 32, 128], P('ctx', 'head')
- loss: float32 [], replicated
- grad_wq: float32 [32, 64, 128], P('head')
- grad_wk: float32 [32, 64, 128], P('head')
The draws below stay inside these ranges and needn't reach their ends.
All inputs are finite; a program needn't handle non-finite values.
Results may differ from the reference program's by a relative error of at most 0.006.
Values may be sent and summed in bfloat16 or wider, within the bound.
No kernel may reach another device: no remote copies, remote signals or barrier semaphores. Data moves between devices by JAX's collectives and lax.ppermute only.
A program may use at most 128 MiB of HBM per device.

```python
import jax
import jax.numpy as jnp
from jax import lax

HEADS = 32
HD = 128
HF = 64
FEAT = 128
WIN = 64
TOK_DEV = 128
TOKENS = 1024


def draw_queries(key, part):
    base = jnp.clip(jax.random.normal(key, (TOKENS, HEADS, HD), jnp.float32), -6.0, 6.0)
    return base.astype(jnp.bfloat16)


def draw_teacher(key, part):
    place = jnp.arange(TOKENS, dtype=jnp.float32) / max(TOKENS - 1, 1)
    base = jnp.clip(jax.random.normal(key, (TOKENS, HEADS, HD), jnp.float32), -6.0, 6.0)
    return (base * (1.0 + 2.0 * place)[:, None, None]).astype(jnp.bfloat16)


def block_scale(stream_key, extent, pieces, low, largest):
    factor_of, own = 1.0, jax.random.fold_in(stream_key, 6)
    for position, parts in pieces:
        steps = jnp.exp(jax.random.uniform(jax.random.fold_in(own, position), (parts,), jnp.float32, low / len(pieces), largest / len(pieces)))
        factor_of = factor_of * jnp.repeat(steps, extent[position] // parts).reshape([-1 if axis == position else 1 for axis in range(len(extent))])
    return factor_of


def noise(stream_key, extent, deviation, reach, split=(), kind=jnp.bfloat16):
    array = jax.random.normal(stream_key, extent, jnp.float32) * deviation
    if len(split) > 0:
        array = block_scale(stream_key, extent, split, -0.22, 0.18) * array
    return jnp.clip(array, min=-reach, max=reach).astype(kind)


def setup_inputs(seed: int = 0) -> dict:
    streams_of = jax.random.split(jax.random.key(seed), 7)
    return {
        "queries": draw_queries(jax.random.fold_in(streams_of[6], 71), 0),
        "keys": noise(streams_of[1], (TOKENS, HEADS, HD), 1.0, 6.0, ((0, 8), (1, 4))),
        "values": noise(streams_of[2], (TOKENS, HEADS, HD), 1.0, 6.0, ((0, 8), (1, 4))),
        "teacher": draw_teacher(jax.random.fold_in(streams_of[6], 71), 0),
        "wq": noise(streams_of[4], (HEADS, HF, HD), HD ** -0.5, 0.5, ((0, 4),)),
        "wk": noise(streams_of[5], (HEADS, HF, HD), HD ** -0.5, 0.5, ((0, 4),)),
    }


def phi(x, w):
    proj = jnp.einsum('thd,hfd->thf', x.astype(jnp.float32), w, precision=lax.Precision.HIGHEST)
    return jnp.concatenate([jax.nn.softmax(proj, axis=-1), jax.nn.softmax(-proj, axis=-1)], axis=-1)

def reference(queries, keys, values, teacher, wq, wk):
    nblock = TOKENS // TOK_DEV
    high = lax.Precision.HIGHEST
    scale = 1.0 / HD ** 0.5
    key_pad = jnp.concatenate([jnp.zeros((WIN, HEADS, HD), jnp.bfloat16), keys], axis=0)
    val_pad = jnp.concatenate([jnp.zeros((WIN, HEADS, HD), jnp.bfloat16), values], axis=0)
    rows = jnp.arange(TOK_DEV, dtype=jnp.int32)[:, None]
    cols = jnp.arange(WIN + TOK_DEV, dtype=jnp.int32)[None, :]
    lower = cols[:, :TOK_DEV] <= rows

    def forward(wq_f, wk_f):

        def step(carry, block):
            state, norm = carry
            first = (block * TOK_DEV).astype(jnp.int32)
            q_blk = lax.dynamic_slice_in_dim(queries, first, TOK_DEV, 0)
            k_blk = lax.dynamic_slice_in_dim(key_pad, first, WIN + TOK_DEV, 0)
            v_blk = lax.dynamic_slice_in_dim(val_pad, first, WIN + TOK_DEV, 0).astype(jnp.float32)
            pos = first - WIN + jnp.arange(WIN + TOK_DEV, dtype=jnp.int32)
            valid = pos >= 0
            early = first + jnp.arange(TOK_DEV, dtype=jnp.int32) < WIN
            inwin = (cols > rows) & (cols <= rows + WIN) & valid[None, :]
            score = jnp.einsum('ihd,chd->hic', q_blk.astype(jnp.float32), k_blk.astype(jnp.float32), precision=high) * scale
            score = jnp.where(inwin[None], score, -jnp.inf)
            top = lax.optimization_barrier(jnp.max(score, axis=-1))
            weight = jnp.where(inwin[None], jnp.exp(score - top[..., None]), 0.0)
            win_num = jnp.einsum('hic,chd->ihd', weight, v_blk, precision=high)
            win_den = lax.optimization_barrier(jnp.sum(weight, axis=-1)).T
            fq = phi(q_blk, wq_f)
            fk = phi(k_blk[:TOK_DEV], wk_f) * valid[:TOK_DEV, None, None].astype(jnp.float32)
            amat = jnp.where(lower[None], jnp.einsum('ihf,chf->hic', fq, fk, precision=high), 0.0)
            lin_num = jnp.einsum('hic,chd->ihd', amat, v_blk[:TOK_DEV], precision=high) + jnp.einsum('ihf,hfd->ihd', fq, state, precision=high)
            lin_den = lax.optimization_barrier(jnp.sum(amat, axis=-1)).T + jnp.einsum('ihf,hf->ih', fq, norm, precision=high)
            top_t = top.T
            win_scale = jnp.where(early[:, None], 1.0, jnp.exp(jnp.minimum(top_t, 0.0)))
            lin_scale = jnp.where(early[:, None], 0.0, jnp.exp(-jnp.maximum(top_t, 0.0)))
            numer = win_scale[..., None] * win_num + lin_scale[..., None] * lin_num
            denom = win_scale * win_den + lin_scale * lin_den
            out = numer / denom[..., None]
            state = state + jnp.einsum('chf,chd->hfd', fk, v_blk[:TOK_DEV], precision=high)
            norm = norm + lax.optimization_barrier(jnp.sum(fk, axis=0))
            return ((state, norm), out)
        init = (jnp.zeros((HEADS, FEAT, HD), jnp.float32), jnp.zeros((HEADS, FEAT), jnp.float32))
        _, outs = lax.scan(step, init, jnp.arange(nblock, dtype=jnp.int32))
        return outs.reshape(TOKENS, HEADS, HD)
    out, pull = jax.vjp(forward, wq.astype(jnp.float32), wk.astype(jnp.float32))
    diff = out - teacher.astype(jnp.float32)
    grad_q, grad_k = pull(2.0 * diff / HD)
    loss = jnp.sum(diff * diff) / (TOKENS * HEADS * HD)
    return (out.astype(jnp.bfloat16), loss, grad_q, grad_k)
```

```python
import functools

import jax
import jax.numpy as jnp
from jax import lax
from jax.experimental import pallas as pl
from jax.experimental.pallas import tpu as pltpu
from jax.sharding import PartitionSpec as P

WIN = 64
QUAD = 4
F32 = jnp.float32
BF16 = jnp.bfloat16


def nt(a, b):
    return lax.dot_general(a, b, (((1,), (1,)), ((), ())), preferred_element_type=F32)


def nn(a, b):
    return lax.dot_general(a, b, (((1,), (0,)), ((), ())), preferred_element_type=F32)


def split2(a):
    high = a.astype(BF16)
    return high, (a - high.astype(F32)).astype(BF16)


def identity(n):
    return (
        lax.broadcasted_iota(jnp.int32, (n, n), 0) == lax.broadcasted_iota(jnp.int32, (n, n), 1)
    ).astype(BF16)


def phi_t(x, w):
    proj = nt(w, x)
    up = jnp.exp(proj - jnp.max(proj, axis=0, keepdims=True))
    down = jnp.exp(jnp.min(proj, axis=0, keepdims=True) - proj)
    up = up * (1.0 / jnp.sum(up, axis=0, keepdims=True))
    down = down * (1.0 / jnp.sum(down, axis=0, keepdims=True))
    return up, down


def phi_pull(up, down, grad):
    half = up.shape[0]
    g_up, g_down = grad[:half], grad[half:]
    d = up * (g_up - jnp.sum(up * g_up, axis=0, keepdims=True))
    return d - down * (g_down - jnp.sum(down * g_down, axis=0, keepdims=True))


def extended(vt):
    row = lax.broadcasted_iota(jnp.int32, (16, vt.shape[1]), 0)
    return jnp.concatenate([vt, (row == 0).astype(BF16)], axis=0)


def to_heads(x_ref, wide):
    tok, heads, d = x_ref.shape
    wide[...] = x_ref[...].astype(F32).reshape(tok * heads, d)
    return [wide[pl.ds(h, tok, stride=heads), :].astype(BF16) for h in range(heads)]


def pack_kernel(where, *refs):
    ins, outs, wide, held = refs[:-6], refs[-6:-2], refs[-2], refs[-1]
    mine = where[0]
    for a, x_ref in enumerate(ins):
        parts = to_heads(x_ref, wide)
        per = len(parts) // QUAD
        for h, part in enumerate(parts):
            held[h // per, a, h % per] = part
    for j, out in enumerate(outs):
        out[...] = held[lax.bitwise_xor(mine, j)]


def key_kernel(where, c0, c1, c2, c3, wk_ref, kv_ref, msg_ref):
    mine = where[0]
    narr, per, tok, d = c0.shape
    for j, c in enumerate((c0, c1, c2, c3)):
        b = lax.bitwise_xor(mine, j)
        kv_ref[:, :, b] = c[...]
    total = QUAD * tok
    eye = identity(d)
    for hh in range(per):
        k = kv_ref[0, hh].reshape(total, d)
        v = kv_ref[1, hh].reshape(total, d)
        up, down = phi_t(k, wk_ref[per * mine + hh])
        feat = jnp.concatenate([up, down], axis=0)
        lane = lax.broadcasted_iota(jnp.int32, feat.shape, 1)
        feat = jnp.where(lane < total - WIN, feat, 0.0).astype(BF16)
        vt = extended(nt(eye, v).astype(BF16))
        state = nt(vt, feat).astype(BF16)
        rows = state.shape[0]
        msg_ref[hh, :rows] = state
        msg_ref[hh, rows : rows + WIN] = k[total - WIN :]
        msg_ref[hh, rows + WIN :] = v[total - WIN :]


def main_kernel(where, kv_ref, c0, c1, c2, c3, msg_ref, wq_ref, wk_ref,
                s0, s1, s2, s3, later_ref, gq_ref, gk_ref, loss_ref, qt, outs, gfk):
    mine, group = where[0], where[1]
    has_past = group > 0
    narr, per, tok, d = c0.shape
    total = QUAD * tok
    for j, c in enumerate((c0, c1, c2, c3)):
        qt[:, :, lax.bitwise_xor(mine, j)] = c[...]
    eye = identity(d)
    scale = 1.0 / d**0.5
    first_key = jnp.where(has_past, tok - WIN, tok)
    loss = jnp.zeros((8, tok), F32)
    for hh in range(per):
        q = qt[0, hh].reshape(total, d)
        teach = nt(eye, qt[1, hh].reshape(total, d))
        halo_k = msg_ref[hh, d + 16 : d + 16 + WIN]
        halo_v = msg_ref[hh, d + 16 + WIN :]
        state = jnp.where(has_past, msg_ref[hh, : d + 16].astype(F32), 0.0)
        state_b = state.astype(BF16)
        state_t = state.T.astype(BF16)
        pad = jnp.zeros((tok - WIN, d), BF16)
        k_all = jnp.concatenate([pad, halo_k, kv_ref[0, hh].reshape(total, d)], axis=0)
        v_all = jnp.concatenate([pad, halo_v, kv_ref[1, hh].reshape(total, d)], axis=0)
        vt_all = extended(nt(eye, v_all).astype(BF16))
        q_up, q_down = phi_t(q, wq_ref[per * mine + hh])
        k_up, k_down = phi_t(k_all, wk_ref[per * mine + hh])
        fq = jnp.concatenate([q_up, q_down], axis=0).astype(BF16)
        fk = jnp.concatenate([k_up, k_down], axis=0)
        fk_rows = fk.T.astype(BF16)
        fk = fk.astype(BF16)
        gfk[...] = jnp.zeros_like(gfk)
        later = jnp.zeros((d + 16, fq.shape[0]), F32)
        gfq = []
        for b in range(QUAD):
            here = slice(b * tok, (b + 1) * tok)
            reach = (b + 2) * tok
            lo = b * tok + WIN
            qb, fqb = q[here], fq[:, here]
            score = nt(k_all[lo:reach], qb) * scale
            row = lax.broadcasted_iota(jnp.int32, score.shape, 0) + lo
            col = lax.broadcasted_iota(jnp.int32, score.shape, 1) + b * tok
            inwin = (row > col + (tok - WIN)) & (row <= col + tok) & (row >= first_key)
            score = jnp.where(inwin, score, -jnp.inf)
            top = jnp.max(score, axis=0, keepdims=True)
            weight = jnp.exp(score - top).astype(BF16)
            weight = jnp.concatenate([jnp.zeros((WIN, tok), BF16), weight], axis=0)
            win = nn(vt_all[:, b * tok : reach], weight)
            row = lax.broadcasted_iota(jnp.int32, (reach, tok), 0)
            col = lax.broadcasted_iota(jnp.int32, (reach, tok), 1) + b * tok
            reached = (row >= first_key) & (row <= col + WIN)
            amat = jnp.where(reached, nn(fk_rows[:reach], fqb), 0.0).astype(BF16)
            lin = nn(vt_all[:, :reach], amat) + nn(state_b, fqb)
            token = lax.broadcasted_iota(jnp.int32, (1, tok), 1) + b * tok
            early = jnp.logical_and(token < WIN, jnp.logical_not(has_past))
            win_scale = jnp.where(early, 1.0, jnp.exp(jnp.minimum(top, 0.0)))
            lin_scale = jnp.where(early, 0.0, jnp.exp(-jnp.maximum(top, 0.0)))
            both = win_scale * win + lin_scale * lin
            denom = both[d : d + 1]
            out = both[:d] / denom
            outs[b, hh] = out.T.astype(BF16)
            diff = out - teach[:, here]
            loss = loss + jnp.sum((diff * diff).reshape(d // 8, 8, tok), axis=0)
            g = diff * (2.0 / d)
            coef = lin_scale / denom
            g_num = coef * g
            g_den = -coef * jnp.sum(g * out, axis=0, keepdims=True)
            pad_row = lax.broadcasted_iota(jnp.int32, (16, tok), 0)
            g_ext = jnp.concatenate([g_num, jnp.where(pad_row == 0, g_den, 0.0)], axis=0).astype(BF16)
            mix = nn(v_all[:reach], g_num.astype(BF16)) + g_den
            mix = jnp.where(reached, mix, 0.0).astype(BF16)
            gfq.append(nn(fk[:, :reach], mix) + nn(state_t, g_ext))
            gfk[:, :reach] += nt(fqb, mix)
            later = later + nt(g_ext, fqb)
        later_ref[hh] = later.astype(BF16)
        for x, up, down, grad, ref in (
            (q, q_up, q_down, jnp.concatenate(gfq, axis=1), gq_ref),
            (k_all, k_up, k_down, gfk[...], gk_ref),
        ):
            high, low = split2(phi_pull(up, down, grad))
            ref[hh] = nn(high, x) + nn(low, x)
    loss_ref[...] = loss
    for j, s in enumerate((s0, s1, s2, s3)):
        s[...] = outs[lax.bitwise_xor(mine, j)]


def put_loss(out_ref, first, loss):
    high, low = split2(loss)
    out_ref[first:] = jnp.concatenate([high, low], axis=0)


def take_loss(ref, first):
    return ref[first : first + 8].astype(F32) + ref[first + 8 : first + 16].astype(F32)


def last_kernel(where, kv_ref, msg_ref, later_ref, wk_ref, gq_ref, gk_ref, l0, l1, l2, l3, out_ref):
    mine, has_past, has_future = where[0], where[1] > 0, where[2] > 0
    per, d = kv_ref.shape[1], kv_ref.shape[-1]
    total = kv_ref.shape[2] * kv_ref.shape[3]
    half = gq_ref.shape[1]
    for hh in range(per):
        after = jnp.where(has_future, later_ref[hh].astype(F32), 0.0)
        after_t = after.T
        k_all = jnp.concatenate([msg_ref[hh, d + 16 : d + 16 + WIN], kv_ref[0, hh].reshape(total, d)], axis=0)
        v_all = jnp.concatenate([msg_ref[hh, d + 16 + WIN :], kv_ref[1, hh].reshape(total, d)], axis=0)
        k_all, v_all = k_all[:total], v_all[:total]
        up, down = phi_t(k_all, wk_ref[per * mine + hh])
        grad = nt(after_t[:, :d].astype(BF16), v_all) + after_t[:, d : d + 1]
        row = lax.broadcasted_iota(jnp.int32, grad.shape, 1)
        grad = jnp.where((row >= WIN) | has_past, grad, 0.0)
        high, low = split2(phi_pull(up, down, grad))
        more = nn(high, k_all) + nn(low, k_all)
        out_ref[hh * half : (hh + 1) * half] = gq_ref[hh].astype(BF16)
        out_ref[(per + hh) * half : (per + hh + 1) * half] = (gk_ref[hh] + more).astype(BF16)
    put_loss(out_ref, 2 * per * half, (l0[...] + l1[...]) + (l2[...] + l3[...]))


def sum_kernel(where, *refs):
    *parts, out_ref = refs
    first = out_ref.shape[0] - 16
    total = sum(part[:first].astype(F32) for part in parts)
    out_ref[:first] = total.astype(BF16)
    put_loss(out_ref, first, sum(take_loss(part, first) for part in parts))


def finish_kernel(entries, where, g0, g1, g2, g3, s0, s1, s2, s3, student, loss, gq, gk, held, wide):
    mine = where[0]
    per, tok, d = s0.shape
    half = gq.shape[1]
    first = 2 * per * half
    l0, l1, l2, l3 = [take_loss(g, first) for g in (g0, g1, g2, g3)]
    loss[0, 0] = jnp.sum((l0 + l1) + (l2 + l3)) / entries
    for j, (g, s) in enumerate(zip((g0, g1, g2, g3), (s0, s1, s2, s3))):
        pair = lax.bitwise_xor(mine, j)
        held[pair] = s[...]
        gq[pl.ds(per * pair, per)] = g[: per * half].astype(F32).reshape(per, half, d)
        gk[pl.ds(per * pair, per)] = g[per * half : first].astype(F32).reshape(per, half, d)
    heads = QUAD * per
    for h in range(heads):
        wide[pl.ds(h, tok, stride=heads), :] = held[h // per, h % per].astype(F32)
    student[...] = wide[...].reshape(tok, heads, d).astype(BF16)


def call(kernel, out_shape, scratch=(), ins=1):
    vmem = pl.BlockSpec(memory_space=pltpu.VMEM)
    return pl.pallas_call(
        kernel,
        out_shape=out_shape,
        in_specs=[pl.BlockSpec(memory_space=pltpu.SMEM)] + [vmem] * ins,
        out_specs=jax.tree.map(
            lambda o: pl.BlockSpec(memory_space=pltpu.SMEM) if o.shape == (1, 1) else vmem, out_shape
        ),
        scratch_shapes=list(scratch),
        compiler_params=pltpu.CompilerParams(vmem_limit_bytes=24 * 2**20),
    )


def shape(*dims, dtype=BF16):
    return jax.ShapeDtypeStruct(dims, dtype)


def flip(x, axis, by):
    return lax.ppermute(x, axis, [(i, i ^ by) for i in range(lax.axis_size(axis))])


def state_over_groups(msg, d, wk_pair, group, groups, members):
    if groups == 2:
        return flip(msg, "ctx", QUAD)
    every = lax.all_gather(msg, "ctx", axis_index_groups=members)
    k, v = every[:, :, d + 16 : d + 16 + WIN], every[:, :, d + 16 + WIN :]
    proj = jnp.einsum("gptd,pfd->gptf", k, wk_pair, preferred_element_type=F32)
    feat = jnp.concatenate([jax.nn.softmax(proj, axis=-1), jax.nn.softmax(-proj, axis=-1)], axis=-1)
    tail = jnp.einsum("gptd,gptf->gpdf", v.astype(F32), feat, precision=lax.Precision.HIGHEST)
    place = jnp.arange(groups)[:, None, None, None]
    norm = jnp.sum(feat, axis=2)[:, :, None, :]
    tail = jnp.concatenate([tail, jnp.pad(norm, ((0, 0), (0, 0), (0, 15), (0, 0)))], axis=2)
    state = jnp.sum(jnp.where(place < group, every[:, :, : d + 16].astype(F32), 0.0), axis=0)
    state = state + jnp.sum(jnp.where(place < group - 1, tail, 0.0), axis=0)
    halo = lax.dynamic_index_in_dim(every, jnp.maximum(group - 1, 0), 0, keepdims=False)
    return jnp.concatenate([state.astype(BF16), halo[:, d + 16 :]], axis=1)


def later_over_groups(later, group, groups, members):
    if groups == 2:
        return flip(later, "ctx", QUAD)
    every = lax.all_gather(later, "ctx", axis_index_groups=members).astype(F32)
    place = jnp.arange(groups)[:, None, None, None]
    return jnp.sum(jnp.where(place > group, every, 0.0), axis=0).astype(BF16)


def sum_over_groups(part, groups, members):
    if groups == 2:
        return [part, flip(part, "ctx", QUAD)]
    every = lax.all_gather(part, "ctx", axis_index_groups=members)
    return [every[g] for g in range(groups)]


def per_device(queries, keys, values, teacher, wq, wk):
    tok, heads, d = queries.shape
    half = wq.shape[1]
    per = heads // QUAD
    place = lax.axis_index("ctx")
    shards = lax.axis_size("ctx")
    groups = shards // QUAD
    members = [[g * QUAD + p for g in range(groups)] for p in range(QUAD)]
    mine, group = place % QUAD, place // QUAD
    where = jnp.stack([mine, group, (group < groups - 1).astype(jnp.int32)]).astype(jnp.int32)

    block = shape(2, per, tok, d)
    pack = call(
        pack_kernel, [block] * QUAD,
        [pltpu.VMEM((tok * heads, d), F32), pltpu.VMEM((QUAD, 2, per, tok, d), BF16)], ins=2,
    )
    kv = pack(where, keys, values)
    kv = [kv[0]] + [flip(kv[j], "ctx", j) for j in range(1, QUAD)]
    qt = pack(where, queries, teacher)
    qt = [qt[0]] + [flip(qt[j], "ctx", j) for j in range(1, QUAD)]

    rows = d + 16 + 2 * WIN
    kv, msg = call(key_kernel, [shape(2, per, QUAD, tok, d), shape(per, rows, d)], ins=5)(where, *kv, wk)
    wk_pair = lax.dynamic_slice_in_dim(wk, per * mine, per, 0) if groups != 2 else None
    msg = state_over_groups(msg, d, wk_pair, group, groups, members)

    grad = shape(per, half, d, dtype=F32)
    out = shape(per, tok, d)
    *out, later, gq, gk, loss = call(
        main_kernel,
        [out] * QUAD + [shape(per, d + 16, 2 * half), grad, grad, shape(8, tok, dtype=F32)],
        [
            pltpu.VMEM((2, per, QUAD, tok, d), BF16),
            pltpu.VMEM((QUAD, per, tok, d), BF16),
            pltpu.VMEM((2 * half, (QUAD + 1) * tok), F32),
        ],
        ins=8,
    )(where, kv, *qt, msg, wq, wk)
    later = later_over_groups(later, group, groups, members)
    losses = [loss] + [flip(loss, "head", j) for j in range(1, lax.axis_size("head"))]
    rows = 2 * per * half + 16
    grads = call(last_kernel, shape(rows, d), ins=10)(where, kv, msg, later, wk, gq, gk, *losses)
    grads = sum_over_groups(grads, groups, members)
    grads = call(sum_kernel, shape(rows, d), ins=len(grads))(where, *grads)
    grads = [grads] + [flip(grads, "ctx", j) for j in range(1, QUAD)]
    out = [out[0]] + [flip(out[j], "ctx", j) for j in range(1, QUAD)]
    entries = tok * shards * heads * lax.axis_size("head") * d
    student, loss, grad_q, grad_k = call(
        functools.partial(finish_kernel, entries),
        [shape(tok, heads, d), shape(1, 1, dtype=F32), shape(heads, half, d, dtype=F32), shape(heads, half, d, dtype=F32)],
        [pltpu.VMEM((QUAD, per, tok, d), BF16), pltpu.VMEM((tok * heads, d), F32)],
        ins=8,
    )(where, *grads, *out)
    return student, loss.reshape(()), grad_q, grad_k


def solution(mesh):
    wide = P("ctx", "head", None)
    narrow = P("head", None, None)
    return jax.shard_map(
        per_device,
        mesh=mesh,
        in_specs=(wide, wide, wide, wide, narrow, narrow),
        out_specs=(wide, P(), narrow, narrow),
        check_vma=False,
    )
```

```python
import functools

import jax
import jax.numpy as jnp
from jax import lax
from jax.experimental import pallas as pl
from jax.experimental.pallas import tpu as pltpu
from jax.sharding import PartitionSpec as P

WIN = 64
QUAD = 4
F32 = jnp.float32
BF16 = jnp.bfloat16
KEY_US, OWN_US, GRAD_US, STUDENT_US = 20.0, 20.0, 20.0, 20.0


def nt(a, b):
    return lax.dot_general(a, b, (((1,), (1,)), ((), ())), preferred_element_type=F32)


def nn(a, b):
    return lax.dot_general(a, b, (((1,), (0,)), ((), ())), preferred_element_type=F32)


def split2(a):
    high = a.astype(BF16)
    return high, (a - high.astype(F32)).astype(BF16)


def identity(n):
    return (
        lax.broadcasted_iota(jnp.int32, (n, n), 0) == lax.broadcasted_iota(jnp.int32, (n, n), 1)
    ).astype(BF16)


def phi_t(x, w):
    proj = nt(w, x)
    up = jnp.exp(proj - jnp.max(proj, axis=0, keepdims=True))
    down = jnp.exp(jnp.min(proj, axis=0, keepdims=True) - proj)
    up = up * (1.0 / jnp.sum(up, axis=0, keepdims=True))
    down = down * (1.0 / jnp.sum(down, axis=0, keepdims=True))
    return up, down


def phi_pull(up, down, grad):
    half = up.shape[0]
    g_up, g_down = grad[:half], grad[half:]
    d = up * (g_up - jnp.sum(up * g_up, axis=0, keepdims=True))
    return d - down * (g_down - jnp.sum(down * g_down, axis=0, keepdims=True))


def extended(vt):
    row = lax.broadcasted_iota(jnp.int32, (16, vt.shape[1]), 0)
    return jnp.concatenate([vt, (row == 0).astype(BF16)], axis=0)


def place_in_group():
    place = lax.axis_index("ctx")
    group = lax.div(place, QUAD)
    return lax.rem(place, QUAD), group > 0, group < lax.axis_size("ctx") // QUAD - 1


def transposed(x):
    return nt(identity(x.shape[1]), x)


def pack_kernel(*refs):
    (x_ref, y_ref), outs, (held_x, held_y, wide, held, sems) = refs[:2], refs[2:-5], refs[-5:]
    copies = [
        pltpu.make_async_copy(src, dst, sems.at[n])
        for n, (src, dst) in enumerate(((x_ref, held_x), (y_ref, held_y)))
    ]
    for copy in copies:
        copy.start()
    mine, _, _ = place_in_group()
    for a, (copy, ref) in enumerate(zip(copies, (held_x, held_y))):
        copy.wait()
        tok, heads, d = ref.shape
        per = heads // QUAD
        wide[a] = ref[...].astype(F32).reshape(tok * heads, d)
        for h in range(heads):
            held[h // per, a, h % per] = wide[a, pl.ds(h, tok, stride=heads), :].astype(BF16)
    for j, out in enumerate(outs):
        out[...] = held[lax.bitwise_xor(mine, j)]


def key_kernel(c0, c1, c2, c3, wk_ref, kv_ref, msg_ref):
    mine, _, _ = place_in_group()
    narr, per, tok, d = c0.shape
    for j, c in enumerate((c0, c1, c2, c3)):
        kv_ref[:, :, lax.bitwise_xor(mine, j)] = c[...]
    total = QUAD * tok
    for hh in range(per):
        k = kv_ref[0, hh].reshape(total, d)
        v = kv_ref[1, hh].reshape(total, d)
        feat = jnp.concatenate(phi_t(k, wk_ref[per * mine + hh]), axis=0)
        lane = lax.broadcasted_iota(jnp.int32, feat.shape, 1)
        feat = jnp.where(lane < total - WIN, feat, 0.0).astype(BF16)
        state = nt(extended(transposed(v).astype(BF16)), feat).astype(BF16)
        rows = state.shape[0]
        msg_ref[hh, :rows] = state
        msg_ref[hh, rows : rows + WIN] = k[total - WIN :]
        msg_ref[hh, rows + WIN :] = v[total - WIN :]


def own_kernel(kv_ref, c0, c1, c2, c3, wq_ref, wk_ref, qt_ref, win_ref, top_ref, lin_ref, fq_ref, up_ref, down_ref):
    mine, _, _ = place_in_group()
    narr, per, tok, d = c0.shape
    total = QUAD * tok
    scale = 1.0 / d**0.5
    for j, c in enumerate((c0, c1, c2, c3)):
        qt_ref[:, :, lax.bitwise_xor(mine, j)] = c[...]
    row = lax.broadcasted_iota(jnp.int32, (tok + WIN, tok), 0)
    col = lax.broadcasted_iota(jnp.int32, (tok + WIN, tok), 1)
    inside = (row > col) & (row <= col + WIN)
    causal = (row <= col)[:tok]
    for hh in range(per):
        q = qt_ref[0, hh].reshape(total, d)
        none = jnp.zeros((WIN, d), BF16)
        k = jnp.concatenate([none, kv_ref[0, hh].reshape(total, d)], axis=0)
        v = jnp.concatenate([none, kv_ref[1, hh].reshape(total, d)], axis=0)
        up, down = phi_t(q, wq_ref[per * mine + hh])
        up_ref[hh], down_ref[hh] = up, down
        fq = jnp.concatenate([up, down], axis=0).astype(BF16)
        fq_ref[hh] = fq
        fk = jnp.concatenate(phi_t(k[:total], wk_ref[per * mine + hh]), axis=0)
        lane = lax.broadcasted_iota(jnp.int32, fk.shape, 1)
        fk = jnp.where(lane >= WIN, fk, 0.0).astype(BF16)
        fk_rows = jnp.concatenate(
            [transposed(fk[:, b * tok : (b + 1) * tok]).astype(BF16) for b in range(QUAD)], axis=0
        )
        vt = extended(transposed(v).astype(BF16))
        for b in range(QUAD):
            lo, hi = b * tok, (b + 1) * tok
            score = nt(k[lo : hi + WIN], q[lo:hi]) * scale
            keep = inside if b else inside & (row >= WIN)
            score = jnp.where(keep, score, -jnp.inf)
            top = jnp.max(score, axis=0, keepdims=True)
            weight = jnp.exp(score - top).astype(BF16)
            win_ref[hh, :, lo:hi] = nn(vt[:, lo : hi + WIN], weight)
            top_ref[hh, :, lo:hi] = jnp.broadcast_to(top, (8, tok))
            amat = nn(fk_rows[:hi], fq[:, lo:hi])
            last = jnp.where(causal, amat[lo:], 0.0)
            amat = jnp.concatenate([amat[:lo], last], axis=0).astype(BF16) if b else last.astype(BF16)
            lin_ref[hh, :, lo:hi] = nn(vt[:, :hi], amat)


def out_kernel(qt_ref, win_ref, top_ref, lin_ref, fq_ref, msg_ref, wk_ref, out_ref, later_ref, grad_ref, loss_ref):
    mine, has_past, _ = place_in_group()
    narr, per, _, tok, d = qt_ref.shape
    total = QUAD * tok
    scale = 1.0 / d**0.5
    token = lax.broadcasted_iota(jnp.int32, (1, total), 1)
    early = jnp.logical_and(token < WIN, jnp.logical_not(has_past))
    row = lax.broadcasted_iota(jnp.int32, (WIN, total), 0)
    col = lax.broadcasted_iota(jnp.int32, (WIN, total), 1)
    loss = jnp.zeros((8, total), F32)
    for hh in range(per):
        fq = fq_ref[hh]
        state = jnp.where(has_past, msg_ref[hh, : d + 16].astype(F32), 0.0).astype(BF16)
        halo_k = msg_ref[hh, d + 16 : d + 16 + WIN]
        vt = extended(transposed(msg_ref[hh, d + 16 + WIN :]).astype(BF16))
        fk = jnp.concatenate(phi_t(halo_k, wk_ref[per * mine + hh]), axis=0)
        fk = jnp.where(has_past, fk, 0.0).astype(BF16)
        amat = nn(transposed(fk).astype(BF16), fq)
        amat = jnp.where(row <= col, amat, 0.0).astype(BF16)
        lin = lin_ref[hh] + nn(state, fq) + nn(vt, amat)
        score = nt(halo_k, qt_ref[0, hh, 0]) * scale
        keep = (row > col)[:, :tok] & has_past
        score = jnp.where(keep, score, -jnp.inf)
        old = top_ref[hh, :1, :tok]
        first = jnp.maximum(old, jnp.max(score, axis=0, keepdims=True))
        weight = jnp.exp(score - first).astype(BF16)
        win = win_ref[hh, :, :tok] * jnp.exp(old - first) + nn(vt, weight)
        win = jnp.concatenate([win, win_ref[hh, :, tok:]], axis=1)
        top = jnp.concatenate([first, top_ref[hh, :1, tok:]], axis=1)
        win_scale = jnp.where(early, 1.0, jnp.exp(jnp.minimum(top, 0.0)))
        lin_scale = jnp.where(early, 0.0, jnp.exp(-jnp.maximum(top, 0.0)))
        both = win_scale * win + lin_scale * lin
        inverse = 1.0 / both[d : d + 1]
        out = both[:d] * inverse
        out_ref[hh] = out.astype(BF16)
        teach = jnp.concatenate([transposed(qt_ref[1, hh, b]) for b in range(QUAD)], axis=1)
        diff = out - teach
        loss = loss + jnp.sum((diff * diff).reshape(d // 8, 8, total), axis=0)
        g = diff * (2.0 / d)
        coef = lin_scale * inverse
        g_num = coef * g
        g_den = -coef * jnp.sum(g * out, axis=0, keepdims=True)
        pad = lax.broadcasted_iota(jnp.int32, (16, total), 0)
        g_ext = jnp.concatenate([g_num, jnp.where(pad == 0, g_den, 0.0)], axis=0).astype(BF16)
        grad_ref[hh] = g_ext
        later_ref[hh] = nt(g_ext, fq).astype(BF16)
    loss_ref[...] = loss


def grad_kernel(kv_ref, qt_ref, msg_ref, grad_ref, out_ref, fq_ref, qup_ref, qdown_ref, wk_ref, diff_ref,
                s0, s1, s2, s3, gq_ref, gk_ref, k_ref, v_ref, kup_ref, kdown_ref, loss_ref, outs):
    loss_ref[...] = sum(diff_ref[:, b * loss_ref.shape[1] : (b + 1) * loss_ref.shape[1]] for b in range(QUAD))
    mine, has_past, _ = place_in_group()
    narr, per, _, tok, d = qt_ref.shape
    total = QUAD * tok
    causal = lax.broadcasted_iota(jnp.int32, (tok, tok), 0) <= lax.broadcasted_iota(jnp.int32, (tok, tok), 1)
    for hh in range(per):
        state = jnp.where(has_past, msg_ref[hh, : d + 16].astype(F32), 0.0).astype(BF16)
        k = jnp.concatenate([msg_ref[hh, d + 16 : d + 16 + WIN], kv_ref[0, hh].reshape(total, d)[: total - WIN]], axis=0)
        v = jnp.concatenate([msg_ref[hh, d + 16 + WIN :], kv_ref[1, hh].reshape(total, d)[: total - WIN]], axis=0)
        k_ref[hh], v_ref[hh] = k, v
        up, down = phi_t(k, wk_ref[per * mine + hh])
        kup_ref[hh], kdown_ref[hh] = up, down
        fk = jnp.concatenate([up, down], axis=0)
        lane = lax.broadcasted_iota(jnp.int32, fk.shape, 1)
        valid = (lane >= WIN) | has_past
        fk = jnp.where(valid, fk, 0.0).astype(BF16)
        fq = fq_ref[hh]
        g_ext = grad_ref[hh]
        g_num, g_den = g_ext[:d], g_ext[d : d + 1].astype(F32)
        grad_q = nn(transposed(state).astype(BF16), g_ext)
        grad_k = []
        for c in range(QUAD):
            lo, hi = c * tok, (c + 1) * tok
            mix = nn(v[lo:hi], g_num[:, lo:]) + g_den[:, lo:]
            first = jnp.where(causal, mix[:, :tok], 0.0)
            mix = (jnp.concatenate([first, mix[:, tok:]], axis=1) if hi < total else first).astype(BF16)
            more = nn(fk[:, lo:hi], mix)
            grad_q = grad_q + (jnp.concatenate([jnp.zeros((more.shape[0], lo), F32), more], axis=1) if c else more)
            grad_k.append(nt(fq[:, lo:], mix))
        grad_k = jnp.where(valid, jnp.concatenate(grad_k, axis=1), 0.0)
        for x, ups, downs, grad, ref in (
            (qt_ref[0, hh].reshape(total, d), qup_ref[hh], qdown_ref[hh], grad_q, gq_ref),
            (k, up, down, grad_k, gk_ref),
        ):
            high, low = split2(phi_pull(ups, downs, grad))
            ref[hh] = nn(high, x) + nn(low, x)
        for b in range(QUAD):
            outs[b, hh] = transposed(out_ref[hh, :, b * tok : (b + 1) * tok]).astype(BF16)
    for j, s in enumerate((s0, s1, s2, s3)):
        s[...] = outs[lax.bitwise_xor(mine, j)]


def put_loss(out_ref, first, loss):
    high, low = split2(loss)
    out_ref[first:] = jnp.concatenate([high, low], axis=0)


def take_loss(ref, first):
    return ref[first : first + 8].astype(F32) + ref[first + 8 : first + 16].astype(F32)


def last_kernel(later_ref, k_ref, v_ref, kup_ref, kdown_ref, gq_ref, gk_ref, l0, l1, l2, l3, out_ref):
    _, has_past, has_future = place_in_group()
    per, total, d = k_ref.shape
    half = gq_ref.shape[1]
    for hh in range(per):
        after = transposed(later_ref[hh])
        grad = nt(after[:, :d].astype(BF16), v_ref[hh]) + after[:, d : d + 1]
        lane = lax.broadcasted_iota(jnp.int32, grad.shape, 1)
        grad = jnp.where(((lane >= WIN) | has_past) & has_future, grad, 0.0)
        high, low = split2(phi_pull(kup_ref[hh], kdown_ref[hh], grad))
        more = nn(high, k_ref[hh]) + nn(low, k_ref[hh])
        out_ref[hh * half : (hh + 1) * half] = gq_ref[hh].astype(BF16)
        out_ref[(per + hh) * half : (per + hh + 1) * half] = (gk_ref[hh] + more).astype(BF16)
    put_loss(out_ref, 2 * per * half, (l0[...] + l1[...]) + (l2[...] + l3[...]))


def sum_kernel(*refs):
    *parts, out_ref = refs
    first = out_ref.shape[0] - 16
    total = sum(part[:first].astype(F32) for part in parts)
    out_ref[:first] = total.astype(BF16)
    put_loss(out_ref, first, sum(take_loss(part, first) for part in parts))


def student_kernel(s0, s1, s2, s3, student, held, wide):
    mine, _, _ = place_in_group()
    per, tok, d = s0.shape
    for j, s in enumerate((s0, s1, s2, s3)):
        held[lax.bitwise_xor(mine, j)] = s[...]
    heads = QUAD * per
    for h in range(heads):
        wide[pl.ds(h, tok, stride=heads), :] = held[h // per, h % per].astype(F32)
    student[...] = wide[...].reshape(tok, heads, d).astype(BF16)


def finish_kernel(entries, g0, g1, g2, g3, loss, gq, gk):
    mine, _, _ = place_in_group()
    heads, half, d = gq.shape
    per = heads // QUAD
    first = 2 * per * half
    l0, l1, l2, l3 = [take_loss(g, first) for g in (g0, g1, g2, g3)]
    loss[0, 0] = jnp.sum((l0 + l1) + (l2 + l3)) / entries
    for j, g in enumerate((g0, g1, g2, g3)):
        here = pl.ds(per * lax.bitwise_xor(mine, j), per)
        gq[here] = g[: per * half].astype(F32).reshape(per, half, d)
        gk[here] = g[per * half : first].astype(F32).reshape(per, half, d)


def call(kernel, out_shape, scratch=(), ins=1, space=pltpu.VMEM, micros=1.0):
    vmem = pl.BlockSpec(memory_space=pltpu.VMEM)
    return pl.pallas_call(
        kernel,
        out_shape=out_shape,
        in_specs=[pl.BlockSpec(memory_space=space)] * ins,
        out_specs=jax.tree.map(
            lambda o: pl.BlockSpec(memory_space=pltpu.SMEM) if o.shape == (1, 1) else vmem, out_shape
        ),
        scratch_shapes=list(scratch),
        cost_estimate=pl.CostEstimate(flops=int(micros * 1e9), bytes_accessed=0, transcendentals=0),
        compiler_params=pltpu.CompilerParams(vmem_limit_bytes=24 * 2**20),
    )


def shape(*dims, dtype=BF16):
    return jax.ShapeDtypeStruct(dims, dtype)


def flip(x, axis, by):
    return lax.ppermute(x, axis, [(i, i ^ by) for i in range(lax.axis_size(axis))])


def state_over_groups(msg, d, wk_pair, group, groups, members):
    if groups == 2:
        return flip(msg, "ctx", QUAD)
    every = lax.all_gather(msg, "ctx", axis_index_groups=members)
    k, v = every[:, :, d + 16 : d + 16 + WIN], every[:, :, d + 16 + WIN :]
    proj = jnp.einsum("gptd,pfd->gptf", k, wk_pair, preferred_element_type=F32)
    feat = jnp.concatenate([jax.nn.softmax(proj, axis=-1), jax.nn.softmax(-proj, axis=-1)], axis=-1)
    tail = jnp.einsum("gptd,gptf->gpdf", v.astype(F32), feat, precision=lax.Precision.HIGHEST)
    place = jnp.arange(groups)[:, None, None, None]
    norm = jnp.sum(feat, axis=2)[:, :, None, :]
    tail = jnp.concatenate([tail, jnp.pad(norm, ((0, 0), (0, 0), (0, 15), (0, 0)))], axis=2)
    state = jnp.sum(jnp.where(place < group, every[:, :, : d + 16].astype(F32), 0.0), axis=0)
    state = state + jnp.sum(jnp.where(place < group - 1, tail, 0.0), axis=0)
    halo = lax.dynamic_index_in_dim(every, jnp.maximum(group - 1, 0), 0, keepdims=False)
    return jnp.concatenate([state.astype(BF16), halo[:, d + 16 :]], axis=1)


def later_over_groups(later, group, groups, members):
    if groups == 2:
        return flip(later, "ctx", QUAD)
    every = lax.all_gather(later, "ctx", axis_index_groups=members).astype(F32)
    place = jnp.arange(groups)[:, None, None, None]
    return jnp.sum(jnp.where(place > group, every, 0.0), axis=0).astype(BF16)


def sum_over_groups(part, groups, members):
    if groups == 2:
        return [part, flip(part, "ctx", QUAD)]
    every = lax.all_gather(part, "ctx", axis_index_groups=members)
    return [every[g] for g in range(groups)]


def per_device(queries, keys, values, teacher, wq, wk):
    tok, heads, d = queries.shape
    half = wq.shape[1]
    per = heads // QUAD
    total = QUAD * tok
    shards = lax.axis_size("ctx")
    groups = shards // QUAD
    group = lax.axis_index("ctx") // QUAD
    members = [[g * QUAD + p for g in range(groups)] for p in range(QUAD)]

    block = shape(2, per, tok, d)
    pack = call(
        pack_kernel, [block] * QUAD,
        [
            pltpu.VMEM((tok, heads, d), BF16),
            pltpu.VMEM((tok, heads, d), BF16),
            pltpu.VMEM((2, tok * heads, d), F32),
            pltpu.VMEM((QUAD, 2, per, tok, d), BF16),
            pltpu.SemaphoreType.DMA((2,)),
        ],
        ins=2, space=pltpu.HBM,
    )
    kv = pack(keys, values)
    kv = [kv[0]] + [flip(kv[j], "ctx", j) for j in range(1, QUAD)]
    qt = pack(queries, teacher)
    qt = [qt[0]] + [flip(qt[j], "ctx", j) for j in range(1, QUAD)]

    rows = d + 16 + 2 * WIN
    kv, msg = call(
        key_kernel, [shape(2, per, QUAD, tok, d), shape(per, rows, d)], ins=5, micros=KEY_US
    )(*kv, wk)
    wk_pair = (
        lax.dynamic_slice_in_dim(wk, per * (lax.axis_index("ctx") % QUAD), per, 0) if groups != 2 else None
    )
    msg = state_over_groups(msg, d, wk_pair, group, groups, members)

    sums = shape(per, d + 16, total, dtype=F32)
    part = shape(per, half, total, dtype=F32)
    grad = shape(per, half, d, dtype=F32)
    qt, win, top, lin, fq, q_up, q_down = call(
        own_kernel,
        [shape(2, per, QUAD, tok, d), sums, shape(per, 8, total, dtype=F32), sums,
         shape(per, 2 * half, total), part, part],
        ins=7, micros=OWN_US,
    )(kv, *qt, wq, wk)
    out, later, g_out, squares = call(
        out_kernel,
        [shape(per, d, total), shape(per, d + 16, 2 * half), shape(per, d + 16, total), shape(8, total, dtype=F32)],
        ins=7, micros=2.0,
    )(qt, win, top, lin, fq, msg, wk)
    later = later_over_groups(later, group, groups, members)
    *out, gq, gk, k, v, k_up, k_down, loss = call(
        grad_kernel,
        [shape(per, tok, d)] * QUAD + [grad, grad, shape(per, total, d), shape(per, total, d), part, part,
         shape(8, tok, dtype=F32)],
        [pltpu.VMEM((QUAD, per, tok, d), BF16)],
        ins=10, micros=GRAD_US,
    )(kv, qt, msg, g_out, out, fq, q_up, q_down, wk, squares)
    losses = [loss] + [flip(loss, "head", j) for j in range(1, lax.axis_size("head"))]
    rows = 2 * per * half + 16
    grads = call(last_kernel, shape(rows, d), ins=11)(later, k, v, k_up, k_down, gq, gk, *losses)
    grads = sum_over_groups(grads, groups, members)
    grads = call(sum_kernel, shape(rows, d), ins=len(grads))(*grads)
    grads = [grads] + [flip(grads, "ctx", j) for j in range(1, QUAD)]
    out = [out[0]] + [flip(out[j], "ctx", j) for j in range(1, QUAD)]
    entries = tok * shards * heads * lax.axis_size("head") * d
    student = call(
        student_kernel, shape(tok, heads, d),
        [pltpu.VMEM((QUAD, per, tok, d), BF16), pltpu.VMEM((tok * heads, d), F32)],
        ins=4, micros=STUDENT_US,
    )(*out)
    whole = shape(heads, half, d, dtype=F32)
    loss, grad_q, grad_k = call(
        functools.partial(finish_kernel, entries), [shape(1, 1, dtype=F32), whole, whole], ins=4
    )(*grads)
    return student, loss.reshape(()), grad_q, grad_k


def solution(mesh):
    wide = P("ctx", "head", None)
    narrow = P("head", None, None)
    return jax.shard_map(
        per_device,
        mesh=mesh,
        in_specs=(wide, wide, wide, wide, narrow, narrow),
        out_specs=(wide, P(), narrow, narrow),
        check_vma=False,
    )
```

```python
import functools

import jax
import jax.numpy as jnp
from jax import lax
from jax.experimental import pallas as pl
from jax.experimental.pallas import tpu as pltpu
from jax.sharding import PartitionSpec as P

WIN = 64
QUAD = 4
F32 = jnp.float32
BF16 = jnp.bfloat16
SPREAD = (0, 3, 1, 2)
KEY_US, OWN_US, GRAD_US, STUDENT_US = 20.0, 20.0, 0.2, 20.0


def nt(a, b):
    return lax.dot_general(a, b, (((1,), (1,)), ((), ())), preferred_element_type=F32)


def nn(a, b):
    return lax.dot_general(a, b, (((1,), (0,)), ((), ())), preferred_element_type=F32)


def split2(a):
    high = a.astype(BF16)
    return high, (a - high.astype(F32)).astype(BF16)


def identity(n):
    return (
        lax.broadcasted_iota(jnp.int32, (n, n), 0) == lax.broadcasted_iota(jnp.int32, (n, n), 1)
    ).astype(BF16)


def phi_t(x, w):
    proj = nt(w, x)
    up = jnp.exp(proj - jnp.max(proj, axis=0, keepdims=True))
    down = jnp.exp(jnp.min(proj, axis=0, keepdims=True) - proj)
    up = up * (1.0 / jnp.sum(up, axis=0, keepdims=True))
    down = down * (1.0 / jnp.sum(down, axis=0, keepdims=True))
    return up, down


def phi_pull(up, down, grad):
    half = up.shape[0]
    g_up, g_down = grad[:half], grad[half:]
    d = up * (g_up - jnp.sum(up * g_up, axis=0, keepdims=True))
    return d - down * (g_down - jnp.sum(down * g_down, axis=0, keepdims=True))


def extended(vt):
    row = lax.broadcasted_iota(jnp.int32, (16, vt.shape[1]), 0)
    return jnp.concatenate([vt, (row == 0).astype(BF16)], axis=0)


def place_in_group():
    place = lax.axis_index("ctx")
    group = lax.div(place, QUAD)
    return lax.rem(place, QUAD), group > 0, group < lax.axis_size("ctx") // QUAD - 1


def transposed(x):
    return nt(identity(x.shape[1]), x)


def pack_kernel(*refs):
    x_ref, outs, (wide, held) = refs[0], refs[-2 - QUAD : -2], refs[-2:]
    mine, _, _ = place_in_group()
    tok, heads, d = x_ref.shape
    tok = tok // 2
    for a in range(2):
        ref = x_ref.at[a * tok : (a + 1) * tok]
        per = heads // QUAD
        wide[a] = ref[...].astype(F32).reshape(tok * heads, d)
        for h in range(heads):
            held[h // per, a, h % per] = wide[a, pl.ds(h, tok, stride=heads), :].astype(BF16)
    for j, out in enumerate(outs):
        out[...] = held[lax.bitwise_xor(mine, j)]


def put_loss(out_ref, first, loss):
    high, low = split2(loss)
    out_ref[first:] = jnp.concatenate([high, low], axis=0)


def take_loss(ref, first):
    return ref[first : first + 8].astype(F32) + ref[first + 8 : first + 16].astype(F32)


def key_kernel(c0, c1, c2, c3, wk_ref, kv_ref, msg_ref):
    mine, _, _ = place_in_group()
    narr, per, tok, d = c0.shape
    for j, c in zip(SPREAD, (c0, c1, c2, c3)):
        kv_ref[:, :, lax.bitwise_xor(mine, j)] = c[...]
    total = QUAD * tok
    for hh in range(per):
        k = kv_ref[0, hh].reshape(total, d)
        v = kv_ref[1, hh].reshape(total, d)
        feat = jnp.concatenate(phi_t(k, wk_ref[per * mine + hh]), axis=0)
        lane = lax.broadcasted_iota(jnp.int32, feat.shape, 1)
        feat = jnp.where(lane < total - WIN, feat, 0.0).astype(BF16)
        state = nt(extended(transposed(v).astype(BF16)), feat).astype(BF16)
        rows = state.shape[0]
        msg_ref[hh, :rows] = state
        msg_ref[hh, rows : rows + WIN] = k[total - WIN :]
        msg_ref[hh, rows + WIN :] = v[total - WIN :]


def own_kernel(kv_ref, c0, c1, c2, c3, wq_ref, wk_ref, qt_ref, teach_ref, win_ref, top_ref, lin_ref, fq_ref, up_ref, down_ref):
    mine, _, _ = place_in_group()
    narr, per, tok, d = c0.shape
    total = QUAD * tok
    scale = 1.0 / d**0.5
    for j, c in zip(SPREAD, (c0, c1, c2, c3)):
        qt_ref[:, :, lax.bitwise_xor(mine, j)] = c[...]
    row = lax.broadcasted_iota(jnp.int32, (tok + WIN, tok), 0)
    col = lax.broadcasted_iota(jnp.int32, (tok + WIN, tok), 1)
    inside = (row > col) & (row <= col + WIN)
    causal = (row <= col)[:tok]
    for hh in range(per):
        q = qt_ref[0, hh].reshape(total, d)
        none = jnp.zeros((WIN, d), BF16)
        k = jnp.concatenate([none, kv_ref[0, hh].reshape(total, d)], axis=0)
        v = jnp.concatenate([none, kv_ref[1, hh].reshape(total, d)], axis=0)
        up, down = phi_t(q, wq_ref[per * mine + hh])
        up_ref[hh], down_ref[hh] = up, down
        fq = jnp.concatenate([up, down], axis=0).astype(BF16)
        fq_ref[hh] = fq
        fk = jnp.concatenate(phi_t(k[:total], wk_ref[per * mine + hh]), axis=0)
        lane = lax.broadcasted_iota(jnp.int32, fk.shape, 1)
        fk = jnp.where(lane >= WIN, fk, 0.0).astype(BF16)
        fk_rows = jnp.concatenate(
            [transposed(fk[:, b * tok : (b + 1) * tok]).astype(BF16) for b in range(QUAD)], axis=0
        )
        vt = extended(transposed(v).astype(BF16))
        for b in range(QUAD):
            lo, hi = b * tok, (b + 1) * tok
            score = nt(k[lo : hi + WIN], q[lo:hi]) * scale
            keep = inside if b else inside & (row >= WIN)
            score = jnp.where(keep, score, -jnp.inf)
            top = jnp.max(score, axis=0, keepdims=True)
            weight = jnp.exp(score - top).astype(BF16)
            win_ref[hh, :, lo:hi] = nn(vt[:, lo : hi + WIN], weight)
            top_ref[hh, :, lo:hi] = jnp.broadcast_to(top, (8, tok))
            amat = nn(fk_rows[:hi], fq[:, lo:hi])
            last = jnp.where(causal, amat[lo:], 0.0)
            amat = jnp.concatenate([amat[:lo], last], axis=0).astype(BF16) if b else last.astype(BF16)
            lin_ref[hh, :, lo:hi] = nn(vt[:, :hi], amat)
            teach_ref[hh, :, lo:hi] = transposed(qt_ref[1, hh, b])


def out_kernel(qt_ref, teach_ref, win_ref, top_ref, lin_ref, fq_ref, msg_ref, wk_ref, s0, s1, s2, s3, later_ref, grad_ref, loss_ref, outs):
    mine, has_past, _ = place_in_group()
    narr, per, _, tok, d = qt_ref.shape
    total = QUAD * tok
    scale = 1.0 / d**0.5
    token = lax.broadcasted_iota(jnp.int32, (1, total), 1)
    early = jnp.logical_and(token < WIN, jnp.logical_not(has_past))
    row = lax.broadcasted_iota(jnp.int32, (WIN, total), 0)
    col = lax.broadcasted_iota(jnp.int32, (WIN, total), 1)
    loss = jnp.zeros((8, total), F32)
    for hh in range(per):
        fq = fq_ref[hh]
        state = jnp.where(has_past, msg_ref[hh, : d + 16].astype(F32), 0.0).astype(BF16)
        halo_k = msg_ref[hh, d + 16 : d + 16 + WIN]
        vt = extended(transposed(msg_ref[hh, d + 16 + WIN :]).astype(BF16))
        fk = jnp.concatenate(phi_t(halo_k, wk_ref[per * mine + hh]), axis=0)
        fk = jnp.where(has_past, fk, 0.0).astype(BF16)
        amat = nn(transposed(fk).astype(BF16), fq)
        amat = jnp.where(row <= col, amat, 0.0).astype(BF16)
        lin = lin_ref[hh] + nn(state, fq) + nn(vt, amat)
        score = nt(halo_k, qt_ref[0, hh, 0]) * scale
        keep = (row > col)[:, :tok] & has_past
        score = jnp.where(keep, score, -jnp.inf)
        old = top_ref[hh, :1, :tok]
        first = jnp.maximum(old, jnp.max(score, axis=0, keepdims=True))
        weight = jnp.exp(score - first).astype(BF16)
        win = win_ref[hh, :, :tok] * jnp.exp(old - first) + nn(vt, weight)
        win = jnp.concatenate([win, win_ref[hh, :, tok:]], axis=1)
        top = jnp.concatenate([first, top_ref[hh, :1, tok:]], axis=1)
        win_scale = jnp.where(early, 1.0, jnp.exp(jnp.minimum(top, 0.0)))
        lin_scale = jnp.where(early, 0.0, jnp.exp(-jnp.maximum(top, 0.0)))
        both = win_scale * win + lin_scale * lin
        inverse = 1.0 / both[d : d + 1]
        out = both[:d] * inverse
        out_rows = out.astype(BF16)
        for b in range(QUAD):
            outs[b, hh] = transposed(out_rows[:, b * tok : (b + 1) * tok]).astype(BF16)
        diff = out - teach_ref[hh]
        loss = loss + jnp.sum((diff * diff).reshape(d // 8, 8, total), axis=0)
        g = diff * (2.0 / d)
        coef = lin_scale * inverse
        g_num = coef * g
        g_den = -coef * jnp.sum(g * out, axis=0, keepdims=True)
        pad = lax.broadcasted_iota(jnp.int32, (16, total), 0)
        g_ext = jnp.concatenate([g_num, jnp.where(pad == 0, g_den, 0.0)], axis=0).astype(BF16)
        grad_ref[hh] = g_ext
        later_ref[hh] = nt(g_ext, fq).astype(BF16)
    loss = sum(loss[:, b * tok : (b + 1) * tok] for b in range(QUAD))
    loss_ref[...] = loss
    for j, s in enumerate((s0, s1, s2, s3)):
        s[...] = outs[lax.bitwise_xor(mine, j)]


def grad_kernel(kv_ref, qt_ref, msg_ref, grad_ref, fq_ref, qup_ref, qdown_ref, wk_ref,
                gq_ref, gk_ref, k_ref, v_ref, kup_ref, kdown_ref):
    mine, has_past, _ = place_in_group()
    narr, per, _, tok, d = qt_ref.shape
    total = QUAD * tok
    causal = lax.broadcasted_iota(jnp.int32, (tok, tok), 0) <= lax.broadcasted_iota(jnp.int32, (tok, tok), 1)
    for hh in range(per):
        state = jnp.where(has_past, msg_ref[hh, : d + 16].astype(F32), 0.0).astype(BF16)
        k = jnp.concatenate([msg_ref[hh, d + 16 : d + 16 + WIN], kv_ref[0, hh].reshape(total, d)[: total - WIN]], axis=0)
        v = jnp.concatenate([msg_ref[hh, d + 16 + WIN :], kv_ref[1, hh].reshape(total, d)[: total - WIN]], axis=0)
        k_ref[hh], v_ref[hh] = k, v
        up, down = phi_t(k, wk_ref[per * mine + hh])
        kup_ref[hh], kdown_ref[hh] = up, down
        fk = jnp.concatenate([up, down], axis=0)
        lane = lax.broadcasted_iota(jnp.int32, fk.shape, 1)
        valid = (lane >= WIN) | has_past
        fk = jnp.where(valid, fk, 0.0).astype(BF16)
        fq = fq_ref[hh]
        g_ext = grad_ref[hh]
        g_num, g_den = g_ext[:d], g_ext[d : d + 1].astype(F32)
        grad_q = nn(transposed(state).astype(BF16), g_ext)
        grad_k = []
        for c in range(QUAD):
            lo, hi = c * tok, (c + 1) * tok
            mix = nn(v[lo:hi], g_num[:, lo:]) + g_den[:, lo:]
            first = jnp.where(causal, mix[:, :tok], 0.0)
            mix = (jnp.concatenate([first, mix[:, tok:]], axis=1) if hi < total else first).astype(BF16)
            more = nn(fk[:, lo:hi], mix)
            grad_q = grad_q + (jnp.concatenate([jnp.zeros((more.shape[0], lo), F32), more], axis=1) if c else more)
            grad_k.append(nt(fq[:, lo:], mix))
        grad_k = jnp.where(valid, jnp.concatenate(grad_k, axis=1), 0.0)
        for x, ups, downs, grad, ref in (
            (qt_ref[0, hh].reshape(total, d), qup_ref[hh], qdown_ref[hh], grad_q, gq_ref),
            (k, up, down, grad_k, gk_ref),
        ):
            high, low = split2(phi_pull(ups, downs, grad))
            ref[hh] = nn(high, x) + nn(low, x)


def last_kernel(later_ref, k_ref, v_ref, kup_ref, kdown_ref, gq_ref, gk_ref, l0, l1, l2, l3, out_ref):
    _, has_past, has_future = place_in_group()
    per, total, d = k_ref.shape
    half = gq_ref.shape[1]
    for hh in range(per):
        after = transposed(later_ref[hh])
        grad = nt(after[:, :d].astype(BF16), v_ref[hh]) + after[:, d : d + 1]
        lane = lax.broadcasted_iota(jnp.int32, grad.shape, 1)
        grad = jnp.where(((lane >= WIN) | has_past) & has_future, grad, 0.0)
        high, low = split2(phi_pull(kup_ref[hh], kdown_ref[hh], grad))
        more = nn(high, k_ref[hh]) + nn(low, k_ref[hh])
        out_ref[hh * half : (hh + 1) * half] = gq_ref[hh].astype(BF16)
        out_ref[(per + hh) * half : (per + hh + 1) * half] = (gk_ref[hh] + more).astype(BF16)
    put_loss(out_ref, 2 * per * half, (l0[...] + l1[...]) + (l2[...] + l3[...]))


def sum_kernel(*refs):
    *parts, out_ref = refs
    first = out_ref.shape[0] - 16
    total = sum(part[:first].astype(F32) for part in parts)
    out_ref[:first] = total.astype(BF16)
    put_loss(out_ref, first, sum(take_loss(part, first) for part in parts))


def student_kernel(s0, s1, s2, s3, student, held, wide):
    mine, _, _ = place_in_group()
    per, tok, d = s0.shape
    for j, s in enumerate((s0, s1, s2, s3)):
        held[lax.bitwise_xor(mine, j)] = s[...]
    heads = QUAD * per
    for h in range(heads):
        wide[pl.ds(h, tok, stride=heads), :] = held[h // per, h % per].astype(F32)
    student[...] = wide[...].reshape(tok, heads, d).astype(BF16)


def finish_kernel(entries, g0, g1, g2, g3, loss, gq, gk):
    mine, _, _ = place_in_group()
    heads, half, d = gq.shape
    per = heads // QUAD
    first = 2 * per * half
    l0, l1, l2, l3 = [take_loss(g, first) for g in (g0, g1, g2, g3)]
    loss[0, 0] = jnp.sum((l0 + l1) + (l2 + l3)) / entries
    for j, g in enumerate((g0, g1, g2, g3)):
        here = pl.ds(per * lax.bitwise_xor(mine, j), per)
        gq[here] = g[: per * half].astype(F32).reshape(per, half, d)
        gk[here] = g[per * half : first].astype(F32).reshape(per, half, d)


def call(kernel, out_shape, scratch=(), ins=1, space=pltpu.VMEM, micros=1.0):
    vmem = pl.BlockSpec(memory_space=pltpu.VMEM)
    return pl.pallas_call(
        kernel,
        out_shape=out_shape,
        in_specs=[pl.BlockSpec(memory_space=space)] * ins,
        out_specs=jax.tree.map(
            lambda o: pl.BlockSpec(memory_space=pltpu.SMEM) if o.shape == (1, 1) else vmem, out_shape
        ),
        scratch_shapes=list(scratch),
        cost_estimate=pl.CostEstimate(flops=int(micros * 1e9), bytes_accessed=0, transcendentals=0),
        compiler_params=pltpu.CompilerParams(vmem_limit_bytes=24 * 2**20),
    )


def shape(*dims, dtype=BF16):
    return jax.ShapeDtypeStruct(dims, dtype)


def flip(x, axis, by):
    return lax.ppermute(x, axis, [(i, i ^ by) for i in range(lax.axis_size(axis))])


def spread(parts):
    return [flip(parts[j], "ctx", j) if j else parts[j] for j in SPREAD]


def state_over_groups(msg, d, wk_pair, group, groups, members):
    if groups == 2:
        return flip(msg, "ctx", QUAD)
    every = lax.all_gather(msg, "ctx", axis_index_groups=members)
    k, v = every[:, :, d + 16 : d + 16 + WIN], every[:, :, d + 16 + WIN :]
    proj = jnp.einsum("gptd,pfd->gptf", k, wk_pair, preferred_element_type=F32)
    feat = jnp.concatenate([jax.nn.softmax(proj, axis=-1), jax.nn.softmax(-proj, axis=-1)], axis=-1)
    tail = jnp.einsum("gptd,gptf->gpdf", v.astype(F32), feat, precision=lax.Precision.HIGHEST)
    place = jnp.arange(groups)[:, None, None, None]
    norm = jnp.sum(feat, axis=2)[:, :, None, :]
    tail = jnp.concatenate([tail, jnp.pad(norm, ((0, 0), (0, 0), (0, 15), (0, 0)))], axis=2)
    state = jnp.sum(jnp.where(place < group, every[:, :, : d + 16].astype(F32), 0.0), axis=0)
    state = state + jnp.sum(jnp.where(place < group - 1, tail, 0.0), axis=0)
    halo = lax.dynamic_index_in_dim(every, jnp.maximum(group - 1, 0), 0, keepdims=False)
    return jnp.concatenate([state.astype(BF16), halo[:, d + 16 :]], axis=1)


def later_over_groups(later, group, groups, members):
    if groups == 2:
        return flip(later, "ctx", QUAD)
    every = lax.all_gather(later, "ctx", axis_index_groups=members).astype(F32)
    place = jnp.arange(groups)[:, None, None, None]
    return jnp.sum(jnp.where(place > group, every, 0.0), axis=0).astype(BF16)


def sum_over_groups(part, groups, members):
    if groups == 2:
        return [part, flip(part, "ctx", QUAD)]
    every = lax.all_gather(part, "ctx", axis_index_groups=members)
    return [every[g] for g in range(groups)]


def per_device(queries, keys, values, teacher, wq, wk):
    tok, heads, d = queries.shape
    half = wq.shape[1]
    per = heads // QUAD
    total = QUAD * tok
    shards = lax.axis_size("ctx")
    groups = shards // QUAD
    group = lax.axis_index("ctx") // QUAD
    members = [[g * QUAD + p for g in range(groups)] for p in range(QUAD)]

    block = shape(2, per, tok, d)
    pack = call(
        pack_kernel, [block] * QUAD,
        [
            pltpu.VMEM((2, tok * heads, d), F32),
            pltpu.VMEM((QUAD, 2, per, tok, d), BF16),
        ],
        ins=1,
    )
    kv = pack(jnp.concatenate([keys, values]))
    kv = spread(kv)
    qt = spread(pack(jnp.concatenate([queries, teacher])))

    rows = d + 16 + 2 * WIN
    kv, msg = call(
        key_kernel, [shape(2, per, QUAD, tok, d), shape(per, rows, d)], ins=5, micros=KEY_US
    )(*kv, wk)
    wk_pair = (
        lax.dynamic_slice_in_dim(wk, per * (lax.axis_index("ctx") % QUAD), per, 0) if groups != 2 else None
    )
    msg = state_over_groups(msg, d, wk_pair, group, groups, members)

    sums = shape(per, d + 16, total, dtype=F32)
    part = shape(per, half, total, dtype=F32)
    grad = shape(per, half, d, dtype=F32)
    qt, teach, win, top, lin, fq, q_up, q_down = call(
        own_kernel,
        [shape(2, per, QUAD, tok, d), shape(per, d, total, dtype=F32), sums, shape(per, 8, total, dtype=F32), sums,
         shape(per, 2 * half, total), part, part],
        ins=7, micros=OWN_US,
    )(kv, *qt, wq, wk)
    block = shape(per, tok, d)
    s0, s1, s2, s3, later, g_out, loss = call(
        out_kernel,
        [block] * QUAD + [shape(per, d + 16, 2 * half), shape(per, d + 16, total), shape(8, tok, dtype=F32)],
        [pltpu.VMEM((QUAD, per, tok, d), BF16)],
        ins=8, micros=2.0,
    )(qt, teach, win, top, lin, fq, msg, wk)
    later = later_over_groups(later, group, groups, members)
    s1, s2, s3 = [flip(s, "ctx", j) for j, s in ((1, s1), (2, s2), (3, s3))]
    losses = [loss] + [flip(loss, "head", j) for j in range(1, lax.axis_size("head"))]
    gq, gk, k, v, k_up, k_down = call(
        grad_kernel,
        [grad, grad, shape(per, total, d), shape(per, total, d), part, part],
        ins=8, micros=GRAD_US,
    )(kv, qt, msg, g_out, fq, q_up, q_down, wk)
    rows = 2 * per * half + 16
    grads = call(last_kernel, shape(rows, d), ins=11)(
        later, k, v, k_up, k_down, gq, gk, *losses
    )
    grads = sum_over_groups(grads, groups, members)
    grads = call(sum_kernel, shape(rows, d), ins=len(grads))(*grads)
    grads = [grads] + [flip(grads, "ctx", j) for j in range(1, QUAD)]
    entries = tok * shards * heads * lax.axis_size("head") * d
    student = call(
        student_kernel, shape(tok, heads, d),
        [pltpu.VMEM((QUAD, per, tok, d), BF16), pltpu.VMEM((tok * heads, d), F32)],
        ins=4, micros=STUDENT_US,
    )(s0, s1, s2, s3)
    whole = shape(heads, half, d, dtype=F32)
    loss, grad_q, grad_k = call(
        functools.partial(finish_kernel, entries), [shape(1, 1, dtype=F32), whole, whole], ins=4
    )(*grads)
    return student, loss.reshape(()), grad_q, grad_k


def solution(mesh):
    wide = P("ctx", "head", None)
    narrow = P("head", None, None)
    return jax.shard_map(
        per_device,
        mesh=mesh,
        in_specs=(wide, wide, wide, wide, narrow, narrow),
        out_specs=(wide, P(), narrow, narrow),
        check_vma=False,
    )
```

```python
import functools

import jax
import jax.numpy as jnp
from jax import lax
from jax.experimental import pallas as pl
from jax.experimental.pallas import tpu as pltpu
from jax.sharding import PartitionSpec as P

WIN = 64
QUAD = 4
F32 = jnp.float32
BF16 = jnp.bfloat16
SPREAD = (0, 3, 1, 2)
KEY_US, FEATURE_US, OWN_US, OUT_US, GRAD_US, STUDENT_US = 20.0, 1.0, 20.0, 1.0, 0.2, 20.0


def nt(a, b):
    return lax.dot_general(a, b, (((1,), (1,)), ((), ())), preferred_element_type=F32)


def nn(a, b):
    return lax.dot_general(a, b, (((1,), (0,)), ((), ())), preferred_element_type=F32)


def split2(a):
    high = a.astype(BF16)
    return high, (a - high.astype(F32)).astype(BF16)


def identity(n):
    return (
        lax.broadcasted_iota(jnp.int32, (n, n), 0) == lax.broadcasted_iota(jnp.int32, (n, n), 1)
    ).astype(BF16)


def phi_t(x, w):
    proj = nt(w, x)
    up = jnp.exp(proj - jnp.max(proj, axis=0, keepdims=True))
    down = jnp.exp(jnp.min(proj, axis=0, keepdims=True) - proj)
    up = up * (1.0 / jnp.sum(up, axis=0, keepdims=True))
    down = down * (1.0 / jnp.sum(down, axis=0, keepdims=True))
    return up, down


def phi_pull(up, down, grad):
    half = up.shape[0]
    g_up, g_down = grad[:half], grad[half:]
    d = up * (g_up - jnp.sum(up * g_up, axis=0, keepdims=True))
    return d - down * (g_down - jnp.sum(down * g_down, axis=0, keepdims=True))


def extended(vt):
    row = lax.broadcasted_iota(jnp.int32, (16, vt.shape[1]), 0)
    return jnp.concatenate([vt, (row == 0).astype(BF16)], axis=0)


def place_in_group():
    place = lax.axis_index("ctx")
    group = lax.div(place, QUAD)
    return lax.rem(place, QUAD), group > 0, group < lax.axis_size("ctx") // QUAD - 1


def transposed(x):
    return nt(identity(x.shape[1]), x)


def pack_kernel(*refs):
    x_ref, outs, (wide, held) = refs[0], refs[-2 - QUAD : -2], refs[-2:]
    mine, _, _ = place_in_group()
    tok, heads, d = x_ref.shape
    tok = tok // 2
    for a in range(2):
        ref = x_ref.at[a * tok : (a + 1) * tok]
        per = heads // QUAD
        wide[a] = ref[...].astype(F32).reshape(tok * heads, d)
        for h in range(heads):
            held[h // per, a, h % per] = wide[a, pl.ds(h, tok, stride=heads), :].astype(BF16)
    for j, out in enumerate(outs):
        out[...] = held[lax.bitwise_xor(mine, j)]


def put_loss(out_ref, first, loss):
    high, low = split2(loss)
    out_ref[first:] = jnp.concatenate([high, low], axis=0)


def take_loss(ref, first):
    return ref[first : first + 8].astype(F32) + ref[first + 8 : first + 16].astype(F32)


def key_kernel(c0, c1, c2, c3, wk_ref, kv_ref, *msg_refs):
    mine, _, _ = place_in_group()
    narr, per, tok, d = c0.shape
    for j, c in zip(SPREAD, (c0, c1, c2, c3)):
        kv_ref[:, :, lax.bitwise_xor(mine, j)] = c[...]
    total = QUAD * tok
    for hh in range(per):
        k = kv_ref[0, hh].reshape(total, d)
        v = kv_ref[1, hh].reshape(total, d)
        feat = jnp.concatenate(phi_t(k, wk_ref[per * mine + hh]), axis=0)
        lane = lax.broadcasted_iota(jnp.int32, feat.shape, 1)
        feat = jnp.where(lane < total - WIN, feat, 0.0).astype(BF16)
        state = nt(extended(transposed(v).astype(BF16)), feat).astype(BF16)
        rows = state.shape[0]
        msg_refs[hh][0, :rows] = state
        msg_refs[hh][0, rows : rows + WIN] = k[total - WIN :]
        msg_refs[hh][0, rows + WIN :] = v[total - WIN :]


def feature_kernel(kv_ref, wk_ref, fk_ref, rows_ref, vt_ref):
    mine, _, _ = place_in_group()
    _, per, _, tok, d = kv_ref.shape
    total = QUAD * tok
    none = jnp.zeros((WIN, d), BF16)
    for hh in range(per):
        k = jnp.concatenate([none, kv_ref[0, hh].reshape(total, d)[: total - WIN]], axis=0)
        v = jnp.concatenate([none, kv_ref[1, hh].reshape(total, d), none], axis=0)
        fk = jnp.concatenate(phi_t(k, wk_ref[per * mine + hh]), axis=0)
        lane = lax.broadcasted_iota(jnp.int32, fk.shape, 1)
        fk = jnp.where(lane >= WIN, fk, 0.0).astype(BF16)
        fk_ref[hh] = fk
        for b in range(QUAD):
            rows_ref[hh, b * tok : (b + 1) * tok] = transposed(fk[:, b * tok : (b + 1) * tok]).astype(BF16)
        vt_ref[hh] = extended(transposed(v).astype(BF16))


def own_kernel(kv_ref, rows_ref, vt_ref, c0, c1, c2, c3, wq_ref, qt_ref, teach_ref, win_ref, top_ref, lin_ref, fq_ref, up_ref, down_ref):
    mine, _, _ = place_in_group()
    narr, per, tok, d = c0.shape
    total = QUAD * tok
    scale = 1.0 / d**0.5
    for j, c in zip(SPREAD, (c0, c1, c2, c3)):
        qt_ref[:, :, lax.bitwise_xor(mine, j)] = c[...]
    row = lax.broadcasted_iota(jnp.int32, (tok + WIN, tok), 0)
    col = lax.broadcasted_iota(jnp.int32, (tok + WIN, tok), 1)
    inside = (row > col) & (row <= col + WIN)
    causal = (row <= col)[:tok]
    for hh in range(per):
        q = qt_ref[0, hh].reshape(total, d)
        none = jnp.zeros((WIN, d), BF16)
        k = jnp.concatenate([none, kv_ref[0, hh].reshape(total, d)], axis=0)
        up, down = phi_t(q, wq_ref[per * mine + hh])
        up_ref[hh], down_ref[hh] = up, down
        fq = jnp.concatenate([up, down], axis=0).astype(BF16)
        fq_ref[hh] = fq
        fk_rows = rows_ref[hh]
        vt = vt_ref[hh]
        for b in range(QUAD):
            lo, hi = b * tok, (b + 1) * tok
            score = nt(k[lo : hi + WIN], q[lo:hi]) * scale
            keep = inside if b else inside & (row >= WIN)
            score = jnp.where(keep, score, -jnp.inf)
            top = jnp.max(score, axis=0, keepdims=True)
            weight = jnp.exp(score - top).astype(BF16)
            win_ref[hh, :, lo:hi] = nn(vt[:, lo : hi + WIN], weight)
            top_ref[hh, :, lo:hi] = jnp.broadcast_to(top, (8, tok))
            amat = nn(fk_rows[:hi], fq[:, lo:hi])
            last = jnp.where(causal, amat[lo:], 0.0)
            amat = jnp.concatenate([amat[:lo], last], axis=0).astype(BF16) if b else last.astype(BF16)
            lin_ref[hh, :, lo:hi] = nn(vt[:, :hi], amat)
            teach_ref[hh, :, lo:hi] = transposed(qt_ref[1, hh, b])


def out_kernel(hh, qt_ref, teach_ref, win_ref, top_ref, lin_ref, fq_ref, msg_ref, wk_ref, *refs):
    *before, out_ref, later_ref, grad_ref, loss_ref = refs
    mine, has_past, _ = place_in_group()
    narr, per, _, tok, d = qt_ref.shape
    total = QUAD * tok
    scale = 1.0 / d**0.5
    token = lax.broadcasted_iota(jnp.int32, (1, total), 1)
    early = jnp.logical_and(token < WIN, jnp.logical_not(has_past))
    row = lax.broadcasted_iota(jnp.int32, (WIN, total), 0)
    col = lax.broadcasted_iota(jnp.int32, (WIN, total), 1)
    fq = fq_ref[hh]
    state = jnp.where(has_past, msg_ref[0, : d + 16].astype(F32), 0.0).astype(BF16)
    halo_k = msg_ref[0, d + 16 : d + 16 + WIN]
    vt = extended(transposed(msg_ref[0, d + 16 + WIN :]).astype(BF16))
    fk = jnp.concatenate(phi_t(halo_k, wk_ref[per * mine + hh]), axis=0)
    fk = jnp.where(has_past, fk, 0.0).astype(BF16)
    amat = nn(transposed(fk).astype(BF16), fq)
    amat = jnp.where(row <= col, amat, 0.0).astype(BF16)
    lin = lin_ref[hh] + nn(state, fq) + nn(vt, amat)
    score = nt(halo_k, qt_ref[0, hh, 0]) * scale
    keep = (row > col)[:, :tok] & has_past
    score = jnp.where(keep, score, -jnp.inf)
    old = top_ref[hh, :1, :tok]
    first = jnp.maximum(old, jnp.max(score, axis=0, keepdims=True))
    weight = jnp.exp(score - first).astype(BF16)
    win = win_ref[hh, :, :tok] * jnp.exp(old - first) + nn(vt, weight)
    win = jnp.concatenate([win, win_ref[hh, :, tok:]], axis=1)
    top = jnp.concatenate([first, top_ref[hh, :1, tok:]], axis=1)
    win_scale = jnp.where(early, 1.0, jnp.exp(jnp.minimum(top, 0.0)))
    lin_scale = jnp.where(early, 0.0, jnp.exp(-jnp.maximum(top, 0.0)))
    both = win_scale * win + lin_scale * lin
    inverse = 1.0 / both[d : d + 1]
    out = both[:d] * inverse
    out_ref[...] = out.astype(BF16)
    diff = out - teach_ref[hh]
    loss = jnp.sum((diff * diff).reshape(d // 8, 8, total), axis=0)
    loss = sum(loss[:, b * tok : (b + 1) * tok] for b in range(QUAD))
    loss_ref[...] = loss + before[1][...] if before else loss
    if before:
        later_ref[:hh] = before[0][...]
    g = diff * (2.0 / d)
    coef = lin_scale * inverse
    g_num = coef * g
    g_den = -coef * jnp.sum(g * out, axis=0, keepdims=True)
    pad = lax.broadcasted_iota(jnp.int32, (16, total), 0)
    g_ext = jnp.concatenate([g_num, jnp.where(pad == 0, g_den, 0.0)], axis=0).astype(BF16)
    grad_ref[...] = g_ext
    later_ref[hh] = nt(g_ext, fq).astype(BF16)


def grad_kernel(per, *refs):
    msg_refs, grad_refs, out_refs = refs[:per], refs[per : 2 * per], refs[2 * per : 3 * per]
    kv_ref, qt_ref, fq_ref, qup_ref, qdown_ref, wk_ref = refs[3 * per : 3 * per + 6]
    s0, s1, s2, s3, gq_ref, gk_ref, k_ref, v_ref, kup_ref, kdown_ref, outs = refs[3 * per + 6 :]
    mine, has_past, _ = place_in_group()
    _, _, _, tok, d = qt_ref.shape
    total = QUAD * tok
    causal = lax.broadcasted_iota(jnp.int32, (tok, tok), 0) <= lax.broadcasted_iota(jnp.int32, (tok, tok), 1)
    for hh in range(per):
        state = jnp.where(has_past, msg_refs[hh][0, : d + 16].astype(F32), 0.0).astype(BF16)
        k = jnp.concatenate([msg_refs[hh][0, d + 16 : d + 16 + WIN], kv_ref[0, hh].reshape(total, d)[: total - WIN]], axis=0)
        v = jnp.concatenate([msg_refs[hh][0, d + 16 + WIN :], kv_ref[1, hh].reshape(total, d)[: total - WIN]], axis=0)
        k_ref[hh], v_ref[hh] = k, v
        up, down = phi_t(k, wk_ref[per * mine + hh])
        kup_ref[hh], kdown_ref[hh] = up, down
        fk = jnp.concatenate([up, down], axis=0)
        lane = lax.broadcasted_iota(jnp.int32, fk.shape, 1)
        valid = (lane >= WIN) | has_past
        fk = jnp.where(valid, fk, 0.0).astype(BF16)
        fq = fq_ref[hh]
        g_ext = grad_refs[hh][...]
        g_num, g_den = g_ext[:d], g_ext[d : d + 1].astype(F32)
        grad_q = nn(transposed(state).astype(BF16), g_ext)
        grad_k = []
        for c in range(QUAD):
            lo, hi = c * tok, (c + 1) * tok
            mix = nn(v[lo:hi], g_num[:, lo:]) + g_den[:, lo:]
            first = jnp.where(causal, mix[:, :tok], 0.0)
            mix = (jnp.concatenate([first, mix[:, tok:]], axis=1) if hi < total else first).astype(BF16)
            more = nn(fk[:, lo:hi], mix)
            grad_q = grad_q + (jnp.concatenate([jnp.zeros((more.shape[0], lo), F32), more], axis=1) if c else more)
            grad_k.append(nt(fq[:, lo:], mix))
        grad_k = jnp.where(valid, jnp.concatenate(grad_k, axis=1), 0.0)
        for x, ups, downs, grad, ref in (
            (qt_ref[0, hh].reshape(total, d), qup_ref[hh], qdown_ref[hh], grad_q, gq_ref),
            (k, up, down, grad_k, gk_ref),
        ):
            high, low = split2(phi_pull(ups, downs, grad))
            ref[hh] = nn(high, x) + nn(low, x)
        for b in range(QUAD):
            outs[b, hh] = transposed(out_refs[hh][:, b * tok : (b + 1) * tok]).astype(BF16)
    for j, s in enumerate((s0, s1, s2, s3)):
        s[...] = outs[lax.bitwise_xor(mine, j)]


def last_kernel(*refs):
    later_ref, k_ref, v_ref, kup_ref, kdown_ref, gq_ref, gk_ref, l0, l1, l2, l3, out_ref = refs
    _, has_past, has_future = place_in_group()
    per, half, d = gq_ref.shape
    for hh in range(per):
        after = transposed(later_ref[hh])
        grad = nt(after[:, :d].astype(BF16), v_ref[hh]) + after[:, d : d + 1]
        lane = lax.broadcasted_iota(jnp.int32, grad.shape, 1)
        grad = jnp.where(((lane >= WIN) | has_past) & has_future, grad, 0.0)
        high, low = split2(phi_pull(kup_ref[hh], kdown_ref[hh], grad))
        more = nn(high, k_ref[hh]) + nn(low, k_ref[hh])
        out_ref[hh * half : (hh + 1) * half] = gq_ref[hh].astype(BF16)
        out_ref[(per + hh) * half : (per + hh + 1) * half] = (gk_ref[hh] + more).astype(BF16)
    put_loss(out_ref, 2 * per * half, (l0[...] + l1[...]) + (l2[...] + l3[...]))


def sum_kernel(*refs):
    *parts, out_ref = refs
    first = out_ref.shape[0] - 16
    total = sum(part[:first].astype(F32) for part in parts)
    out_ref[:first] = total.astype(BF16)
    put_loss(out_ref, first, sum(take_loss(part, first) for part in parts))


def student_kernel(s0, s1, s2, s3, student, held, wide):
    mine, _, _ = place_in_group()
    per, tok, d = s0.shape
    for j, s in enumerate((s0, s1, s2, s3)):
        held[lax.bitwise_xor(mine, j)] = s[...]
    heads = QUAD * per
    for h in range(heads):
        wide[pl.ds(h, tok, stride=heads), :] = held[h // per, h % per].astype(F32)
    student[...] = wide[...].reshape(tok, heads, d).astype(BF16)


def finish_kernel(entries, g0, g1, g2, g3, loss, gq, gk):
    mine, _, _ = place_in_group()
    heads, half, d = gq.shape
    per = heads // QUAD
    first = 2 * per * half
    l0, l1, l2, l3 = [take_loss(g, first) for g in (g0, g1, g2, g3)]
    loss[0, 0] = jnp.sum((l0 + l1) + (l2 + l3)) / entries
    for j, g in enumerate((g0, g1, g2, g3)):
        here = pl.ds(per * lax.bitwise_xor(mine, j), per)
        gq[here] = g[: per * half].astype(F32).reshape(per, half, d)
        gk[here] = g[per * half : first].astype(F32).reshape(per, half, d)


def call(kernel, out_shape, scratch=(), ins=1, space=pltpu.VMEM, micros=1.0):
    vmem = pl.BlockSpec(memory_space=pltpu.VMEM)
    return pl.pallas_call(
        kernel,
        out_shape=out_shape,
        in_specs=[pl.BlockSpec(memory_space=space)] * ins,
        out_specs=jax.tree.map(
            lambda o: pl.BlockSpec(memory_space=pltpu.SMEM) if o.shape == (1, 1) else vmem, out_shape
        ),
        scratch_shapes=list(scratch),
        cost_estimate=pl.CostEstimate(flops=int(micros * 1e9), bytes_accessed=0, transcendentals=0),
        compiler_params=pltpu.CompilerParams(vmem_limit_bytes=24 * 2**20),
    )


def shape(*dims, dtype=BF16):
    return jax.ShapeDtypeStruct(dims, dtype)


def flip(x, axis, by):
    return lax.ppermute(x, axis, [(i, i ^ by) for i in range(lax.axis_size(axis))])


def spread(parts):
    return [flip(parts[j], "ctx", j) if j else parts[j] for j in SPREAD]


def state_over_groups(msg, d, wk, head, group, groups, members):
    if groups == 2:
        return flip(msg, "ctx", QUAD)
    wk_pair = lax.dynamic_slice_in_dim(wk, head, 1, 0)
    every = lax.all_gather(msg, "ctx", axis_index_groups=members)
    k, v = every[:, :, d + 16 : d + 16 + WIN], every[:, :, d + 16 + WIN :]
    proj = jnp.einsum("gptd,pfd->gptf", k, wk_pair, preferred_element_type=F32)
    feat = jnp.concatenate([jax.nn.softmax(proj, axis=-1), jax.nn.softmax(-proj, axis=-1)], axis=-1)
    tail = jnp.einsum("gptd,gptf->gpdf", v.astype(F32), feat, precision=lax.Precision.HIGHEST)
    place = jnp.arange(groups)[:, None, None, None]
    norm = jnp.sum(feat, axis=2)[:, :, None, :]
    tail = jnp.concatenate([tail, jnp.pad(norm, ((0, 0), (0, 0), (0, 15), (0, 0)))], axis=2)
    state = jnp.sum(jnp.where(place < group, every[:, :, : d + 16].astype(F32), 0.0), axis=0)
    state = state + jnp.sum(jnp.where(place < group - 1, tail, 0.0), axis=0)
    halo = lax.dynamic_index_in_dim(every, jnp.maximum(group - 1, 0), 0, keepdims=False)
    return jnp.concatenate([state.astype(BF16), halo[:, d + 16 :]], axis=1)


def later_over_groups(later, group, groups, members):
    if groups == 2:
        return flip(later, "ctx", QUAD)
    every = lax.all_gather(later, "ctx", axis_index_groups=members).astype(F32)
    place = jnp.arange(groups)[:, None, None, None]
    return jnp.sum(jnp.where(place > group, every, 0.0), axis=0).astype(BF16)


def sum_over_groups(part, groups, members):
    if groups == 2:
        return [part, flip(part, "ctx", QUAD)]
    every = lax.all_gather(part, "ctx", axis_index_groups=members)
    return [every[g] for g in range(groups)]


def per_device(queries, keys, values, teacher, wq, wk):
    tok, heads, d = queries.shape
    half = wq.shape[1]
    per = heads // QUAD
    total = QUAD * tok
    shards = lax.axis_size("ctx")
    groups = shards // QUAD
    group = lax.axis_index("ctx") // QUAD
    members = [[g * QUAD + p for g in range(groups)] for p in range(QUAD)]

    block = shape(2, per, tok, d)
    pack = call(
        pack_kernel, [block] * QUAD,
        [
            pltpu.VMEM((2, tok * heads, d), F32),
            pltpu.VMEM((QUAD, 2, per, tok, d), BF16),
        ],
        ins=1,
    )
    kv = pack(jnp.concatenate([keys, values]))
    kv = spread(kv)
    qt = spread(pack(jnp.concatenate([queries, teacher])))

    rows = d + 16 + 2 * WIN
    kv, *msgs = call(
        key_kernel, [shape(2, per, QUAD, tok, d)] + [shape(1, rows, d)] * per, ins=5, micros=KEY_US
    )(*kv, wk)
    first = per * (lax.axis_index("ctx") % QUAD)
    msgs = [state_over_groups(msg, d, wk, first + hh, group, groups, members) for hh, msg in enumerate(msgs)]

    sums = shape(per, d + 16, total, dtype=F32)
    part = shape(per, half, total, dtype=F32)
    grad = shape(per, half, d, dtype=F32)
    fk, fk_rows, vt = call(
        feature_kernel,
        [shape(per, 2 * half, total), shape(per, total, 2 * half), shape(per, d + 16, total + 2 * WIN)],
        ins=2, micros=FEATURE_US,
    )(kv, wk)
    qt, teach, win, top, lin, fq, q_up, q_down = call(
        own_kernel,
        [shape(2, per, QUAD, tok, d), shape(per, d, total, dtype=F32), sums, shape(per, 8, total, dtype=F32), sums,
         shape(per, 2 * half, total), part, part],
        ins=8, micros=OWN_US,
    )(kv, fk_rows, vt, *qt, wq)
    outs, g_outs, before = [], [], ()
    for hh in range(per):
        out, later, g_out, loss = call(
            functools.partial(out_kernel, hh),
            [shape(d, total), shape(hh + 1, d + 16, 2 * half), shape(d + 16, total), shape(8, tok, dtype=F32)],
            ins=8 + len(before), micros=OUT_US,
        )(qt, teach, win, top, lin, fq, msgs[hh], wk, *before)
        outs.append(out)
        g_outs.append(g_out)
        before = (later, loss)
    later = later_over_groups(later, group, groups, members)
    losses = [loss] + [flip(loss, "head", j) for j in range(1, lax.axis_size("head"))]
    s0, s1, s2, s3, gq, gk, k, v, k_up, k_down = call(
        functools.partial(grad_kernel, per),
        [shape(per, tok, d)] * QUAD + [grad, grad, shape(per, total, d), shape(per, total, d), part, part],
        [pltpu.VMEM((QUAD, per, tok, d), BF16)],
        ins=3 * per + 6, micros=GRAD_US,
    )(*msgs, *g_outs, *outs, kv, qt, fq, q_up, q_down, wk)
    s1, s2, s3 = [flip(s, "ctx", j) for j, s in ((1, s1), (2, s2), (3, s3))]
    rows = 2 * per * half + 16
    grads = call(last_kernel, shape(rows, d), ins=11)(
        later, k, v, k_up, k_down, gq, gk, *losses
    )
    grads = sum_over_groups(grads, groups, members)
    grads = call(sum_kernel, shape(rows, d), ins=len(grads))(*grads)
    grads = [grads] + [flip(grads, "ctx", j) for j in range(1, QUAD)]
    entries = tok * shards * heads * lax.axis_size("head") * d
    student = call(
        student_kernel, shape(tok, heads, d),
        [pltpu.VMEM((QUAD, per, tok, d), BF16), pltpu.VMEM((tok * heads, d), F32)],
        ins=4, micros=STUDENT_US,
    )(s0, s1, s2, s3)
    whole = shape(heads, half, d, dtype=F32)
    loss, grad_q, grad_k = call(
        functools.partial(finish_kernel, entries), [shape(1, 1, dtype=F32), whole, whole], ins=4
    )(*grads)
    return student, loss.reshape(()), grad_q, grad_k


def solution(mesh):
    wide = P("ctx", "head", None)
    narrow = P("head", None, None)
    return jax.shard_map(
        per_device,
        mesh=mesh,
        in_specs=(wide, wide, wide, wide, narrow, narrow),
        out_specs=(wide, P(), narrow, narrow),
        check_vma=False,
    )
```

```python
import functools

import jax
import jax.numpy as jnp
from jax import lax
from jax.experimental import pallas as pl
from jax.experimental.pallas import tpu as pltpu
from jax.sharding import PartitionSpec as P

WIN = 64
QUAD = 4
F32 = jnp.float32
BF16 = jnp.bfloat16
KEYS_FIRST = (0, 3, 1, 2)
QUERIES_FIRST = (0, 1, 3, 2)
KEY_US, FEATURE_US, OWN_US, OUT_US, GRAD_US, STUDENT_US = 20.0, 1.0, 20.0, 1.0, 0.2, 20.0


def nt(a, b):
    return lax.dot_general(a, b, (((1,), (1,)), ((), ())), preferred_element_type=F32)


def nn(a, b):
    return lax.dot_general(a, b, (((1,), (0,)), ((), ())), preferred_element_type=F32)


def split2(a):
    high = a.astype(BF16)
    return high, (a - high.astype(F32)).astype(BF16)


def identity(n):
    return (
        lax.broadcasted_iota(jnp.int32, (n, n), 0) == lax.broadcasted_iota(jnp.int32, (n, n), 1)
    ).astype(BF16)


def phi_t(x, w):
    proj = nt(w, x)
    up = jnp.exp(proj - jnp.max(proj, axis=0, keepdims=True))
    down = jnp.exp(jnp.min(proj, axis=0, keepdims=True) - proj)
    up = up * (1.0 / jnp.sum(up, axis=0, keepdims=True))
    down = down * (1.0 / jnp.sum(down, axis=0, keepdims=True))
    return up, down


def phi_pull(up, down, grad):
    half = up.shape[0]
    g_up, g_down = grad[:half], grad[half:]
    d = up * (g_up - jnp.sum(up * g_up, axis=0, keepdims=True))
    return d - down * (g_down - jnp.sum(down * g_down, axis=0, keepdims=True))


def extended(vt):
    row = lax.broadcasted_iota(jnp.int32, (16, vt.shape[1]), 0)
    return jnp.concatenate([vt, (row == 0).astype(BF16)], axis=0)


def place_in_group():
    place = lax.axis_index("ctx")
    group = lax.div(place, QUAD)
    return lax.rem(place, QUAD), group > 0, group < lax.axis_size("ctx") // QUAD - 1


def transposed(x):
    return nt(identity(x.shape[1]), x)


def pack_kernel(*refs):
    x_ref, outs, (wide, held) = refs[0], refs[-2 - QUAD : -2], refs[-2:]
    mine, _, _ = place_in_group()
    tok, heads, d = x_ref.shape
    tok = tok // 2
    for a in range(2):
        ref = x_ref.at[a * tok : (a + 1) * tok]
        per = heads // QUAD
        wide[a] = ref[...].astype(F32).reshape(tok * heads, d)
        for h in range(heads):
            held[h // per, a, h % per] = wide[a, pl.ds(h, tok, stride=heads), :].astype(BF16)
    for j, out in enumerate(outs):
        out[...] = held[lax.bitwise_xor(mine, j)]


def norm_rows(norm):
    high, low = split2(norm)
    row = lax.broadcasted_iota(jnp.int32, (16, norm.shape[1]), 0)
    both = jnp.where(row == 0, high.astype(F32), jnp.where(row == 1, low.astype(F32), 0.0))
    return both.astype(BF16)


def put_loss(out_ref, first, loss):
    high, low = split2(loss)
    out_ref[first:] = jnp.concatenate([high, low], axis=0)


def take_loss(ref, first):
    both = ref[first : first + 16].astype(F32)
    return both[:8] + both[8:]


def key_kernel(c0, c1, c2, c3, wk_ref, kv_ref, *msg_refs):
    mine, _, _ = place_in_group()
    narr, per, tok, d = c0.shape
    for j, c in zip(KEYS_FIRST, (c0, c1, c2, c3)):
        kv_ref[:, :, lax.bitwise_xor(mine, j)] = c[...]
    total = QUAD * tok
    for hh in range(per):
        k = kv_ref[0, hh].reshape(total, d)
        v = kv_ref[1, hh].reshape(total, d)
        feat = jnp.concatenate(phi_t(k, wk_ref[per * mine + hh]), axis=0)
        lane = lax.broadcasted_iota(jnp.int32, feat.shape, 1)
        feat = jnp.where(lane < total - WIN, feat, 0.0).astype(BF16)
        state = nt(extended(transposed(v).astype(BF16)), feat)
        rows = state.shape[0]
        msg_refs[hh][0, :d] = state[:d].astype(BF16)
        msg_refs[hh][0, d:rows] = norm_rows(state[d : d + 1])
        msg_refs[hh][0, rows : rows + WIN] = k[total - WIN :]
        msg_refs[hh][0, rows + WIN :] = v[total - WIN :]


def feature_kernel(kv_ref, wk_ref, fk_ref, rows_ref, vt_ref):
    mine, _, _ = place_in_group()
    _, per, _, tok, d = kv_ref.shape
    total = QUAD * tok
    none = jnp.zeros((WIN, d), BF16)
    for hh in range(per):
        k = jnp.concatenate([none, kv_ref[0, hh].reshape(total, d)[: total - WIN]], axis=0)
        v = jnp.concatenate([none, kv_ref[1, hh].reshape(total, d), none], axis=0)
        fk = jnp.concatenate(phi_t(k, wk_ref[per * mine + hh]), axis=0)
        lane = lax.broadcasted_iota(jnp.int32, fk.shape, 1)
        fk = jnp.where(lane >= WIN, fk, 0.0).astype(BF16)
        fk_ref[hh] = fk
        for b in range(QUAD):
            rows_ref[hh, b * tok : (b + 1) * tok] = transposed(fk[:, b * tok : (b + 1) * tok]).astype(BF16)
        vt_ref[hh] = extended(transposed(v).astype(BF16))


def own_kernel(kv_ref, rows_ref, vt_ref, c0, c1, c2, c3, wq_ref, qt_ref, teach_ref, win_ref, top_ref, lin_ref, fq_ref, up_ref, down_ref):
    mine, _, _ = place_in_group()
    narr, per, tok, d = c0.shape
    total = QUAD * tok
    scale = 1.0 / d**0.5
    for j, c in zip(QUERIES_FIRST, (c0, c1, c2, c3)):
        qt_ref[:, :, lax.bitwise_xor(mine, j)] = c[...]
    row = lax.broadcasted_iota(jnp.int32, (tok + WIN, tok), 0)
    col = lax.broadcasted_iota(jnp.int32, (tok + WIN, tok), 1)
    inside = (row > col) & (row <= col + WIN)
    wide = 2 * tok
    causal = lax.broadcasted_iota(jnp.int32, (wide, wide), 0) <= lax.broadcasted_iota(jnp.int32, (wide, wide), 1)
    for hh in range(per):
        q = qt_ref[0, hh].reshape(total, d)
        none = jnp.zeros((WIN, d), BF16)
        k = jnp.concatenate([none, kv_ref[0, hh].reshape(total, d)], axis=0)
        up, down = phi_t(q, wq_ref[per * mine + hh])
        up_ref[hh], down_ref[hh] = up, down
        fq = jnp.concatenate([up, down], axis=0).astype(BF16)
        fq_ref[hh] = fq
        fk_rows = rows_ref[hh]
        vt = vt_ref[hh]
        for b in range(QUAD):
            lo, hi = b * tok, (b + 1) * tok
            score = nt(k[lo : hi + WIN], q[lo:hi]) * scale
            keep = inside if b else inside & (row >= WIN)
            score = jnp.where(keep, score, -jnp.inf)
            top = jnp.max(score, axis=0, keepdims=True)
            weight = jnp.exp(score - top).astype(BF16)
            win_ref[hh, :, lo:hi] = nn(vt[:, lo : hi + WIN], weight)
            top_ref[hh, :, lo:hi] = jnp.broadcast_to(top, (8, tok))
            teach_ref[hh, :, lo:hi] = transposed(qt_ref[1, hh, b])
        for lo in range(0, total, wide):
            hi = lo + wide
            amat = nn(fk_rows[:hi], fq[:, lo:hi])
            last = jnp.where(causal, amat[lo:], 0.0)
            amat = jnp.concatenate([amat[:lo], last], axis=0).astype(BF16) if lo else last.astype(BF16)
            lin_ref[hh, :, lo:hi] = nn(vt[:, :hi], amat)


def out_kernel(hh, qt_ref, teach_ref, win_ref, top_ref, lin_ref, fq_ref, msg_ref, wk_ref, *refs):
    *before, out_ref, later_ref, grad_ref, loss_ref = refs
    mine, has_past, _ = place_in_group()
    narr, per, _, tok, d = qt_ref.shape
    total = QUAD * tok
    scale = 1.0 / d**0.5
    token = lax.broadcasted_iota(jnp.int32, (1, total), 1)
    early = jnp.logical_and(token < WIN, jnp.logical_not(has_past))
    row = lax.broadcasted_iota(jnp.int32, (WIN, total), 0)
    col = lax.broadcasted_iota(jnp.int32, (WIN, total), 1)
    fq = fq_ref[hh]
    state = jnp.where(has_past, msg_ref[0, : d + 16].astype(F32), 0.0).astype(BF16)
    halo_k = msg_ref[0, d + 16 : d + 16 + WIN]
    vt = extended(transposed(msg_ref[0, d + 16 + WIN :]).astype(BF16))
    fk = jnp.concatenate(phi_t(halo_k, wk_ref[per * mine + hh]), axis=0)
    fk = jnp.where(has_past, fk, 0.0).astype(BF16)
    amat = lax.dot_general(fk, fq, (((0,), (0,)), ((), ())), preferred_element_type=F32)
    amat = jnp.where(row <= col, amat, 0.0).astype(BF16)
    lin = lin_ref[hh] + nn(state, fq) + nn(vt, amat)
    score = nt(halo_k, qt_ref[0, hh, 0]) * scale
    keep = (row > col)[:, :tok] & has_past
    score = jnp.where(keep, score, -jnp.inf)
    old = top_ref[hh, :1, :tok]
    first = jnp.maximum(old, jnp.max(score, axis=0, keepdims=True))
    weight = jnp.exp(score - first).astype(BF16)
    win = win_ref[hh, :, :tok] * jnp.exp(old - first) + nn(vt, weight)
    win = jnp.concatenate([win, win_ref[hh, :, tok:]], axis=1)
    top = jnp.concatenate([first, top_ref[hh, :1, tok:]], axis=1)
    win_scale = jnp.where(early, 1.0, jnp.exp(jnp.minimum(top, 0.0)))
    lin_scale = jnp.where(early, 0.0, jnp.exp(-jnp.maximum(top, 0.0)))
    both = win_scale * win + lin_scale * lin
    inverse = 1.0 / (both[d : d + 1] + both[d + 1 : d + 2])
    out = both[:d] * inverse
    out_ref[...] = out.astype(BF16)
    diff = out - teach_ref[hh]
    loss = jnp.sum((diff * diff).reshape(d // 8, 8, total), axis=0)
    loss = sum(loss[:, b * tok : (b + 1) * tok] for b in range(QUAD))
    loss_ref[...] = loss + before[1][...] if before else loss
    if before:
        later_ref[:hh] = before[0][...]
    g = diff * (2.0 / d)
    coef = lin_scale * inverse
    g_num = coef * g
    g_den = -coef * jnp.sum(g * out, axis=0, keepdims=True)
    pad = lax.broadcasted_iota(jnp.int32, (16, total), 0)
    g_ext = jnp.concatenate([g_num, jnp.where(pad <= 1, g_den, 0.0)], axis=0).astype(BF16)
    grad_ref[...] = g_ext
    feat = fq.shape[0]
    later_ref[hh, :feat] = nt(fq, g_ext[:d]).astype(BF16)
    later_ref[hh, feat:] = norm_rows(nt(g_ext[d:], fq)[:1])


def grad_kernel(per, *refs):
    msg_refs, grad_refs, out_refs = refs[:per], refs[per : 2 * per], refs[2 * per : 3 * per]
    kv_ref, qt_ref, fq_ref, qup_ref, qdown_ref, wk_ref = refs[3 * per : 3 * per + 6]
    s0, s1, s2, s3, gq_ref, gk_ref, k_ref, v_ref, kup_ref, kdown_ref, outs = refs[3 * per + 6 :]
    mine, has_past, _ = place_in_group()
    _, _, _, tok, d = qt_ref.shape
    total = QUAD * tok
    wide = 2 * tok
    causal = lax.broadcasted_iota(jnp.int32, (wide, wide), 0) <= lax.broadcasted_iota(jnp.int32, (wide, wide), 1)
    for hh in range(per):
        state = jnp.where(has_past, msg_refs[hh][0, : d + 16].astype(F32), 0.0).astype(BF16)
        k = jnp.concatenate([msg_refs[hh][0, d + 16 : d + 16 + WIN], kv_ref[0, hh].reshape(total, d)[: total - WIN]], axis=0)
        v = jnp.concatenate([msg_refs[hh][0, d + 16 + WIN :], kv_ref[1, hh].reshape(total, d)[: total - WIN]], axis=0)
        k_ref[hh], v_ref[hh] = k, v
        up, down = phi_t(k, wk_ref[per * mine + hh])
        kup_ref[hh], kdown_ref[hh] = up, down
        fk = jnp.concatenate([up, down], axis=0)
        lane = lax.broadcasted_iota(jnp.int32, fk.shape, 1)
        valid = (lane >= WIN) | has_past
        fk = jnp.where(valid, fk, 0.0).astype(BF16)
        fq = fq_ref[hh]
        g_ext = grad_refs[hh][...]
        g_num, g_den = g_ext[:d], g_ext[d:].astype(F32)[:1]
        grad_q = nn(transposed(state).astype(BF16), g_ext)
        grad_k = []
        for lo in range(0, total, wide):
            hi = lo + wide
            mix = nn(v[lo:hi], g_num[:, lo:]) + g_den[:, lo:]
            first = jnp.where(causal, mix[:, :wide], 0.0)
            mix = (jnp.concatenate([first, mix[:, wide:]], axis=1) if hi < total else first).astype(BF16)
            more = nn(fk[:, lo:hi], mix)
            grad_q = grad_q + (jnp.concatenate([jnp.zeros((more.shape[0], lo), F32), more], axis=1) if lo else more)
            grad_k.append(nt(fq[:, lo:], mix))
        grad_k = jnp.where(valid, jnp.concatenate(grad_k, axis=1), 0.0)
        for x, ups, downs, grad, ref in (
            (qt_ref[0, hh].reshape(total, d), qup_ref[hh], qdown_ref[hh], grad_q, gq_ref),
            (k, up, down, grad_k, gk_ref),
        ):
            high, low = split2(phi_pull(ups, downs, grad))
            ref[hh] = nn(high, x) + nn(low, x)
        for b in range(QUAD):
            outs[b, hh] = transposed(out_refs[hh][:, b * tok : (b + 1) * tok]).astype(BF16)
    for j, s in enumerate((s0, s1, s2, s3)):
        s[...] = outs[lax.bitwise_xor(mine, j)]


def last_kernel(*refs):
    later_ref, k_ref, v_ref, kup_ref, kdown_ref, gq_ref, gk_ref, l0, l1, l2, l3, out_ref = refs
    _, has_past, has_future = place_in_group()
    per, half, d = gq_ref.shape
    for hh in range(per):
        feat = 2 * half
        norm = transposed(later_ref[hh, feat:])
        grad = nt(later_ref[hh, :feat], v_ref[hh]) + (norm[:, :1] + norm[:, 1:2])
        lane = lax.broadcasted_iota(jnp.int32, grad.shape, 1)
        grad = jnp.where(((lane >= WIN) | has_past) & has_future, grad, 0.0)
        high, low = split2(phi_pull(kup_ref[hh], kdown_ref[hh], grad))
        more = nn(high, k_ref[hh]) + nn(low, k_ref[hh])
        out_ref[hh * half : (hh + 1) * half] = gq_ref[hh].astype(BF16)
        out_ref[(per + hh) * half : (per + hh + 1) * half] = (gk_ref[hh] + more).astype(BF16)
    put_loss(out_ref, 2 * per * half, (l0[...] + l1[...]) + (l2[...] + l3[...]))


def sum_kernel(*refs):
    *parts, out_ref = refs
    first = out_ref.shape[0] - 16
    total = sum(part[:first].astype(F32) for part in parts)
    out_ref[:first] = total.astype(BF16)
    put_loss(out_ref, first, sum(take_loss(part, first) for part in parts))


def student_kernel(s0, s1, s2, s3, student, held, wide):
    mine, _, _ = place_in_group()
    per, tok, d = s0.shape
    for j, s in enumerate((s0, s1, s2, s3)):
        held[lax.bitwise_xor(mine, j)] = s[...]
    heads = QUAD * per
    for h in range(heads):
        wide[pl.ds(h, tok, stride=heads), :] = held[h // per, h % per].astype(F32)
    student[...] = wide[...].reshape(tok, heads, d).astype(BF16)


def finish_kernel(entries, g0, g1, g2, g3, loss, gq, gk):
    mine, _, _ = place_in_group()
    heads, half, d = gq.shape
    per = heads // QUAD
    first = 2 * per * half
    l0, l1, l2, l3 = [take_loss(g, first) for g in (g0, g1, g2, g3)]
    loss[0, 0] = jnp.sum((l0 + l1) + (l2 + l3)) / entries
    for j, g in enumerate((g0, g1, g2, g3)):
        here = pl.ds(per * lax.bitwise_xor(mine, j), per)
        gq[here] = g[: per * half].astype(F32).reshape(per, half, d)
        gk[here] = g[per * half : first].astype(F32).reshape(per, half, d)


def call(kernel, out_shape, scratch=(), ins=1, space=pltpu.VMEM, micros=1.0):
    vmem = pl.BlockSpec(memory_space=pltpu.VMEM)
    return pl.pallas_call(
        kernel,
        out_shape=out_shape,
        in_specs=[pl.BlockSpec(memory_space=space)] * ins,
        out_specs=jax.tree.map(
            lambda o: pl.BlockSpec(memory_space=pltpu.SMEM) if o.shape == (1, 1) else vmem, out_shape
        ),
        scratch_shapes=list(scratch),
        cost_estimate=pl.CostEstimate(flops=int(micros * 1e9), bytes_accessed=0, transcendentals=0),
        compiler_params=pltpu.CompilerParams(vmem_limit_bytes=24 * 2**20),
    )


def shape(*dims, dtype=BF16):
    return jax.ShapeDtypeStruct(dims, dtype)


def flip(x, axis, by):
    return lax.ppermute(x, axis, [(i, i ^ by) for i in range(lax.axis_size(axis))])


def spread(parts, order):
    return [flip(parts[j], "ctx", j) if j else parts[j] for j in order]


def state_over_groups(msg, d, wk, head, group, groups, members):
    if groups == 2:
        return flip(msg, "ctx", QUAD)
    wk_pair = lax.dynamic_slice_in_dim(wk, head, 1, 0)
    every = lax.all_gather(msg, "ctx", axis_index_groups=members)
    k, v = every[:, :, d + 16 : d + 16 + WIN], every[:, :, d + 16 + WIN :]
    proj = jnp.einsum("gptd,pfd->gptf", k, wk_pair, preferred_element_type=F32)
    feat = jnp.concatenate([jax.nn.softmax(proj, axis=-1), jax.nn.softmax(-proj, axis=-1)], axis=-1)
    tail = jnp.einsum("gptd,gptf->gpdf", v.astype(F32), feat, precision=lax.Precision.HIGHEST)
    place = jnp.arange(groups)[:, None, None, None]
    norm = jnp.sum(feat, axis=2)[:, :, None, :]
    tail = jnp.concatenate([tail, jnp.pad(norm, ((0, 0), (0, 0), (0, 15), (0, 0)))], axis=2)
    state = jnp.sum(jnp.where(place < group, every[:, :, : d + 16].astype(F32), 0.0), axis=0)
    state = state + jnp.sum(jnp.where(place < group - 1, tail, 0.0), axis=0)
    halo = lax.dynamic_index_in_dim(every, jnp.maximum(group - 1, 0), 0, keepdims=False)
    norm = norm_rows(state[0, d : d + 1] + state[0, d + 1 : d + 2])[None]
    return jnp.concatenate([state[:, :d].astype(BF16), norm, halo[:, d + 16 :]], axis=1)


def later_over_groups(later, group, groups, members):
    if groups == 2:
        return flip(later, "ctx", QUAD)
    every = lax.all_gather(later, "ctx", axis_index_groups=members).astype(F32)
    place = jnp.arange(groups)[:, None, None, None]
    state = jnp.sum(jnp.where(place > group, every, 0.0), axis=0)
    feat = state.shape[1] - 16
    norm = jnp.stack([norm_rows(head[feat : feat + 1] + head[feat + 1 : feat + 2]) for head in state])
    return jnp.concatenate([state[:, :feat].astype(BF16), norm], axis=1)


def sum_over_groups(part, groups, members):
    if groups == 2:
        return [part, flip(part, "ctx", QUAD)]
    every = lax.all_gather(part, "ctx", axis_index_groups=members)
    return [every[g] for g in range(groups)]


def per_device(queries, keys, values, teacher, wq, wk):
    tok, heads, d = queries.shape
    half = wq.shape[1]
    per = heads // QUAD
    total = QUAD * tok
    shards = lax.axis_size("ctx")
    groups = shards // QUAD
    group = lax.axis_index("ctx") // QUAD
    members = [[g * QUAD + p for g in range(groups)] for p in range(QUAD)]

    block = shape(2, per, tok, d)
    pack = call(
        pack_kernel, [block] * QUAD,
        [
            pltpu.VMEM((2, tok * heads, d), F32),
            pltpu.VMEM((QUAD, 2, per, tok, d), BF16),
        ],
        ins=1,
    )
    kv = spread(pack(jnp.concatenate([keys, values])), KEYS_FIRST)
    qt = spread(pack(jnp.concatenate([queries, teacher])), QUERIES_FIRST)

    rows = d + 16 + 2 * WIN
    kv, *msgs = call(
        key_kernel, [shape(2, per, QUAD, tok, d)] + [shape(1, rows, d)] * per, ins=5, micros=KEY_US
    )(*kv, wk)
    first = per * (lax.axis_index("ctx") % QUAD)
    msgs = [state_over_groups(msg, d, wk, first + hh, group, groups, members) for hh, msg in enumerate(msgs)]

    sums = shape(per, d + 16, total, dtype=F32)
    part = shape(per, half, total, dtype=F32)
    grad = shape(per, half, d, dtype=F32)
    fk, fk_rows, vt = call(
        feature_kernel,
        [shape(per, 2 * half, total), shape(per, total, 2 * half), shape(per, d + 16, total + 2 * WIN)],
        ins=2, micros=FEATURE_US,
    )(kv, wk)
    qt, teach, win, top, lin, fq, q_up, q_down = call(
        own_kernel,
        [shape(2, per, QUAD, tok, d), shape(per, d, total, dtype=F32), sums, shape(per, 8, total, dtype=F32), sums,
         shape(per, 2 * half, total), part, part],
        ins=8, micros=OWN_US,
    )(kv, fk_rows, vt, *qt, wq)
    outs, g_outs, before = [], [], ()
    for hh in range(per):
        out, later, g_out, loss = call(
            functools.partial(out_kernel, hh),
            [shape(d, total), shape(hh + 1, 2 * half + 16, d), shape(d + 16, total), shape(8, tok, dtype=F32)],
            ins=8 + len(before), micros=OUT_US,
        )(qt, teach, win, top, lin, fq, msgs[hh], wk, *before)
        outs.append(out)
        g_outs.append(g_out)
        before = (later, loss)
    later = later_over_groups(later, group, groups, members)
    losses = [loss] + [flip(loss, "head", j) for j in range(1, lax.axis_size("head"))]
    s0, s1, s2, s3, gq, gk, k, v, k_up, k_down = call(
        functools.partial(grad_kernel, per),
        [shape(per, tok, d)] * QUAD + [grad, grad, shape(per, total, d), shape(per, total, d), part, part],
        [pltpu.VMEM((QUAD, per, tok, d), BF16)],
        ins=3 * per + 6, micros=GRAD_US,
    )(*msgs, *g_outs, *outs, kv, qt, fq, q_up, q_down, wk)
    s1, s2, s3 = [flip(s, "ctx", j) for j, s in ((1, s1), (2, s2), (3, s3))]
    rows = 2 * per * half + 16
    grads = call(last_kernel, shape(rows, d), ins=11)(
        later, k, v, k_up, k_down, gq, gk, *losses
    )
    grads = sum_over_groups(grads, groups, members)
    grads = call(sum_kernel, shape(rows, d), ins=len(grads))(*grads)
    grads = [grads] + [flip(grads, "ctx", j) for j in range(1, QUAD)]
    entries = tok * shards * heads * lax.axis_size("head") * d
    student = call(
        student_kernel, shape(tok, heads, d),
        [pltpu.VMEM((QUAD, per, tok, d), BF16), pltpu.VMEM((tok * heads, d), F32)],
        ins=4, micros=STUDENT_US,
    )(s0, s1, s2, s3)
    whole = shape(heads, half, d, dtype=F32)
    loss, grad_q, grad_k = call(
        functools.partial(finish_kernel, entries), [shape(1, 1, dtype=F32), whole, whole], ins=4
    )(*grads)
    return student, loss.reshape(()), grad_q, grad_k


def solution(mesh):
    wide = P("ctx", "head", None)
    narrow = P("head", None, None)
    return jax.shard_map(
        per_device,
        mesh=mesh,
        in_specs=(wide, wide, wide, wide, narrow, narrow),
        out_specs=(wide, P(), narrow, narrow),
        check_vma=False,
    )
```
